256 devices in a mesh: sec: 4 (over z_lo, core), seq: 64 (over y, x, z_hi).
Axes of the slice: x: 4, y: 4, z: 8 (z_hi: 4, z_lo: 2; z = z_hi * 2 + z_lo), core: 2. Of those that a mesh axis runs over, the one named last changes fastest.
Arguments:
- queries: bfloat16 [4, 6144, 4096], P('sec', 'seq'), may hold values from -6 to 6
- keys: bfloat16 [4, 6144, 4096], P('sec', 'seq'), may hold values from -6 to 6
- values: bfloat16 [4, 6144, 4096], P('sec', 'seq'), may hold values from -6 to 6
- query_gain: float32 [4096], replicated, may hold values from 0.1 to 1.9
- key_gain: float32 [4096], replicated, may hold values from 0.1 to 1.9
- noisy: float32 [4, 6144, 64], P('sec', 'seq'), may hold values from -6 to 6
- head_weight: bfloat16 [4096, 64], replicated, may hold values from -3 to 3
- conv_in_weight: bfloat16 [3, 3, 3, 16, 384], replicated, may hold values from -0.3125 to 0.3125
- conv_in_bias: float32 [384], replicated, may hold values from -3 to 3
- vae_gain: float32 [384], replicated, may hold values from 0.1 to 1.9
- conv_weight: bfloat16 [3, 3, 3, 384, 384], replicated, may hold values from -0.0625 to 0.0625
Outputs:
- latents: float32 [4, 6144, 64], P('sec', 'seq')
- decoded: bfloat16 [4, 8, 128, 24, 384], P(None, 'sec', 'seq')
The draws below stay inside these ranges and needn't reach their ends.
All inputs are finite; a program needn't handle non-finite values.
Results may differ from the reference program's by a relative error of at most 0.013.
The reference program's roundings to bfloat16 on the way count: a program that leaves them out, or rounds other values in their place, can miss the bound.
Values may be sent and summed in bfloat16 or wider, within the bound.
A program may use at most 64 MiB of HBM per device.

```python
import math
import jax
import jax.numpy as jnp
from jax import lax

HEADS = 32
HEAD_DIM = 128
LAT_CH = 16
VAE_CH = 384
PCOLS = 12
REQS = 4
FRAMES = 8
TOKENS = 6144
HL = 128
WL = 24
N_SEQ = 64


def draw_queries(key, part):
    key = jax.random.fold_in(key, 1)
    result = jnp.clip(jax.random.normal(key, (REQS, TOKENS, HEADS * HEAD_DIM), jnp.float32), -6.0, 6.0)
    return result.astype(jnp.bfloat16)


def draw_keys(key, part):
    key = jax.random.fold_in(key, 2)
    result = jnp.clip(jax.random.normal(key, (REQS, TOKENS, HEADS * HEAD_DIM), jnp.float32), -6.0, 6.0)
    return result.astype(jnp.bfloat16)


def steps_of(stream_key, dims, split, smallest, high):
    def one(position, parts):
        steps = jax.random.uniform(jax.random.fold_in(jax.random.fold_in(stream_key, 6), position), (parts,), jnp.float32, smallest / len(split), high / len(split))
        return jnp.repeat(jnp.exp(steps), dims[position] // parts).reshape((-1,) + (1,) * (len(dims) - position - 1))

    level = one(*split[0])
    for cut in split[1:]:
        level = level * one(*cut)
    return level


def normal_values(rng, dims, width, limit, cuts=(), held_as=jnp.bfloat16):
    factor_of = steps_of(rng, dims, cuts, -0.22, 0.18) if cuts else 1.0
    values = jax.random.normal(rng, dims, jnp.float32) * width * factor_of
    return jnp.minimum(jnp.maximum(values, -limit), limit).astype(held_as)


def setup_inputs(seed: int = 0) -> dict:
    key_of = jax.random.split(jax.random.key(seed), 12)
    return {
        "queries": draw_queries(jax.random.fold_in(key_of[11], 71), 0),
        "keys": draw_keys(jax.random.fold_in(key_of[11], 71), 0),
        "values": normal_values(key_of[2], (REQS, TOKENS, HEADS * HEAD_DIM), 1.0, 6.0, ((0, 4), (1, 64))),
        "query_gain": jnp.clip(1.0 + 0.18 * jax.random.normal(key_of[3], (HEADS * HEAD_DIM,), jnp.float32), 0.1, 1.9),
        "key_gain": jnp.clip(1.0 + 0.18 * jax.random.normal(key_of[4], (HEADS * HEAD_DIM,), jnp.float32), 0.1, 1.9),
        "noisy": normal_values(key_of[5], (REQS, TOKENS, 4 * LAT_CH), 1.0, 6.0, ((0, 4), (1, 64)), jnp.float32),
        "head_weight": normal_values(key_of[6], (HEADS * HEAD_DIM, 4 * LAT_CH), 0.5, 3.0),
        "conv_in_weight": normal_values(key_of[7], (3, 3, 3, LAT_CH, VAE_CH), (27 * LAT_CH) ** -0.5, 0.3125),
        "conv_in_bias": normal_values(key_of[8], (VAE_CH,), 0.5, 3.0, (), jnp.float32),
        "vae_gain": jnp.clip(1.0 + 0.18 * jax.random.normal(key_of[9], (VAE_CH,), jnp.float32), 0.1, 1.9),
        "conv_weight": normal_values(key_of[10], (3, 3, 3, VAE_CH, VAE_CH), (27 * VAE_CH) ** -0.5, 0.0625),
    }


eps = 1e-06

def rms_scale(values_in, gain):
    floats = values_in.astype(jnp.float32)
    meansq = lax.optimization_barrier(jnp.mean(floats * floats, axis=-1, keepdims=True))
    return floats * lax.rsqrt(meansq + eps) * gain

def causal_conv(video, weight):
    padded = jnp.pad(video, ((0, 0), (2, 0), (1, 1), (1, 1), (0, 0)))
    flat_weight = weight.reshape(-1, weight.shape[-1])
    row_count = video.shape[2]
    col_count = video.shape[3]
    outputs = []
    for frame in range(video.shape[1]):
        pieces = []
        for time_off in range(3):
            for row_off in range(3):
                for col_off in range(3):
                    pieces.append(padded[:, frame + time_off, row_off:row_off + row_count, col_off:col_off + col_count, :])
        outputs.append(jnp.dot(jnp.concatenate(pieces, -1), flat_weight, preferred_element_type=jnp.float32))
    return jnp.stack(outputs, 1)

def reference(queries, keys, values, query_gain, key_gain, noisy, head_weight, conv_in_weight, conv_in_bias, vae_gain, conv_weight):
    channels = HEADS * HEAD_DIM
    q_norm = rms_scale(queries, query_gain).astype(jnp.bfloat16)
    k_norm = rms_scale(keys, key_gain).astype(jnp.bfloat16)

    def heads_first(array):
        return array.reshape(REQS, TOKENS, HEADS, HEAD_DIM).transpose(0, 2, 1, 3).reshape(REQS * HEADS, TOKENS, HEAD_DIM)
    factor = 1.0 / math.sqrt(HEAD_DIM)

    def one_head(triple):
        query_head, key_head, value_head = triple
        scores = jnp.dot(query_head, key_head.T, preferred_element_type=jnp.float32) * factor
        maxima = lax.optimization_barrier(jnp.max(scores, axis=-1, keepdims=True))
        exp_scores = jnp.exp(scores - maxima)
        totals = lax.optimization_barrier(jnp.sum(exp_scores, axis=-1, keepdims=True))
        summed = jnp.dot(exp_scores.astype(jnp.bfloat16), value_head, preferred_element_type=jnp.float32)
        return (summed / totals).astype(jnp.bfloat16)
    attended = lax.map(one_head, (heads_first(q_norm), heads_first(k_norm), heads_first(values)))
    tokens_out = attended.reshape(REQS, HEADS, TOKENS, HEAD_DIM).transpose(0, 2, 1, 3).reshape(REQS * TOKENS, channels)
    velocity = jnp.dot(tokens_out, head_weight, preferred_element_type=jnp.float32)
    latents = noisy + velocity.reshape(REQS, TOKENS, 4 * LAT_CH)
    video = latents.astype(jnp.bfloat16).reshape(REQS, N_SEQ, FRAMES, PCOLS, 2, 2, LAT_CH)
    video = video.transpose(0, 2, 1, 4, 3, 5, 6).reshape(REQS, FRAMES, HL, WL, LAT_CH)
    hidden = (causal_conv(video, conv_in_weight) + conv_in_bias).astype(jnp.bfloat16)
    act = jax.nn.silu(rms_scale(hidden, vae_gain)).astype(jnp.bfloat16)
    decoded = (hidden.astype(jnp.float32) + causal_conv(act, conv_weight)).astype(jnp.bfloat16)
    return (latents, decoded)
```

```python
import functools
import math

import jax
import jax.numpy as jnp
import numpy as np
from jax import lax
from jax.experimental import pallas as pl
from jax.experimental.pallas import tpu as pltpu
from jax.sharding import PartitionSpec as P

HEADS = 32
HEAD_DIM = 128
ROWS = 96
HALF = ROWS // 2
SEQ = 64
SEC = 4
STEPS = 32
PER_CHUNK = 4
CHUNKS = STEPS // PER_CHUNK
QB = PER_CHUNK * ROWS
N_QB = STEPS // PER_CHUNK
KC = PER_CHUNK * ROWS
PCOLS = 12
RC = SEC * PCOLS
CH = 384
EPS = 1e-06
MESH = pl.DeviceIdType.MESH
NT = (((1,), (1,)), ((), ()))
LOG2E = 1.0 / math.log(2.0)


def offsets(i):
    b, c = lax.rem(lax.div(i, 4), 4), lax.rem(i, 4)
    dy = lax.rem(lax.div(i, 16) + lax.div(c, 2), 2)
    return dy, lax.rem(b + c, 4), c


def place_after(j, i):
    dy, dx, dz = offsets(i)
    y = lax.rem(lax.div(j, 16) + dy, 2)
    x = lax.rem(lax.rem(lax.div(j, 4), 4) + dx, 4)
    z = lax.rem(lax.rem(j, 4) + dz, 4)
    return y * 16 + x * 4 + z


def place_before(h, i):
    dy, dx, dz = offsets(i)
    y = lax.rem(lax.div(h, 16) + 2 - dy, 2)
    x = lax.rem(lax.rem(lax.div(h, 4), 4) + 4 - dx, 4)
    z = lax.rem(lax.rem(h, 4) + 4 - dz, 4)
    return y * 16 + x * 4 + z


def gather_constants():
    rows = np.zeros((3, 4 * RC, 4 * RC), np.float32)
    lanes = np.zeros((3, 128, 256), np.float32)
    for k in range(3):
        for f in range(4):
            for r in range(SEC):
                for c in range(PCOLS):
                    if 0 <= c + k - 1 < PCOLS:
                        rows[k, (f * SEC + r) * PCOLS + c, (r * 4 + f) * PCOLS + c + k - 1] = 1
    for half in range(2):
        for i in range(2):
            for tap, (k, j) in enumerate(((0, 1), (1, 0), (1, 1), (2, 0))):
                for ch in range(16):
                    lanes[k, half * 64 + i * 32 + j * 16 + ch, half * 128 + i * 64 + tap * 16 + ch] = 1
    return rows, lanes.reshape(384, 256)


def kernel(
    q_ref, k_ref, v_ref, qg_ref, kg_ref, noisy_ref, hw_ref, win_ref, bias_ref, vg_ref, w_ref, rowsel_ref, lanesel_ref,
    lat_ref, dec_ref,
    qsrc, kvsrc, qbuf, kvbuf, sibbuf, acc, m_s, l_s, s_a, s_b, obuf, vbuf,
    xsrc, xrecv, xf, lhs, hid, tap, wbig, wconv, w_h, cacc,
    ssq, sskv, ssf, sso, ssx, rq, rkv, rf, ro, rx, lsem,
):
    sec, p = lax.axis_index("sec"), lax.axis_index("seq")
    z_lo, core = lax.div(sec, 2), lax.rem(sec, 2)
    part, place = lax.div(p, 32), lax.rem(p, 32)

    def target(h):
        return (2 * z_lo + 1 - part, h + 32 * core)

    def source(j):
        return (2 * z_lo + part, j + 32 * (1 - core))

    sibling = (2 * z_lo + 1 - core, p)

    def beside(d):
        return lax.rem(p + SEQ + d, SEQ)

    barrier = pltpu.get_barrier_semaphore()

    def greet(i, _):
        pl.semaphore_signal(barrier, inc=1, device_id=target(place_after(place, i)), device_id_type=MESH)
        pl.semaphore_signal(barrier, inc=1, device_id=source(place_before(place, i)), device_id_type=MESH)
        return 0

    lax.fori_loop(0, STEPS, greet, 0)
    pl.semaphore_signal(barrier, inc=1, device_id=sibling, device_id_type=MESH)
    for d in (-1, 0, 1):
        for s in range(1, SEC) if d == 0 else range(SEC):
            pl.semaphore_signal(barrier, inc=1, device_id=(lax.rem(sec + s, SEC), beside(d)), device_id_type=MESH)

    w_copy = pltpu.make_async_copy(w_ref, wconv, lsem.at[0])
    w_copy.start()
    hw_copy = pltpu.make_async_copy(hw_ref.at[pl.ds(pl.multiple_of(place * HEAD_DIM, HEAD_DIM), HEAD_DIM)], w_h, lsem.at[1])
    hw_copy.start()

    def normed(ref, gain_ref, factor, store):
        def some(t, _):
            rows = pl.ds(pl.multiple_of(t * 16, 16), 16)
            x = ref[rows, :].astype(jnp.float32)
            scale = lax.rsqrt(jnp.mean(x * x, axis=-1, keepdims=True) + EPS)
            for h in range(HEADS):
                cols = slice(h * HEAD_DIM, (h + 1) * HEAD_DIM)
                y = x[:, cols] * scale * gain_ref[:, cols]
                store(h, rows, (y if factor is None else y * factor).astype(jnp.bfloat16))
            return 0

        lax.fori_loop(0, ROWS // 16, some, 0)

    def store_q(h, rows, y):
        qsrc[h, rows, :] = y

    def store_k(h, rows, y):
        kvsrc[h, 0, rows, :] = y

    normed(q_ref, qg_ref, LOG2E / math.sqrt(HEAD_DIM), store_q)
    pl.semaphore_wait(barrier, 2 * STEPS + 1 + 3 * SEC - 1)

    def send_q(i, _):
        h = place_after(place, i)
        pltpu.make_async_remote_copy(
            src_ref=qsrc.at[h], dst_ref=qbuf.at[i], send_sem=ssq, recv_sem=rq, device_id=target(h), device_id_type=MESH
        ).start()
        return 0

    lax.fori_loop(0, STEPS, send_q, 0)
    for h in range(HEADS):
        kvsrc[h, 1] = v_ref[:, h * HEAD_DIM : (h + 1) * HEAD_DIM]
    normed(k_ref, kg_ref, None, store_k)

    def send_kv(i, _):
        h = place_after(place, i)
        pltpu.make_async_remote_copy(
            src_ref=kvsrc.at[h],
            dst_ref=kvbuf.at[i],
            send_sem=sskv,
            recv_sem=rkv.at[lax.div(i, PER_CHUNK)],
            device_id=target(h),
            device_id_type=MESH,
        ).start()
        return 0

    lax.fori_loop(0, STEPS, send_kv, 0)

    wbig[...] = jnp.zeros_like(wbig)
    for a in range(3):
        for b in range(3):
            block = win_ref[pl.ds((a * 3 + b) * 48, 48), :]
            for i in range(2):
                for j in range(2):
                    wbig[pl.ds(a * 256 + (b + i) * 64 + j * 16, 48), pl.ds((i * 2 + j) * CH, CH)] = block
    xf[pl.ds(0, 4)] = jnp.zeros((4,) + xf.shape[1:], jnp.bfloat16)
    acc[...] = jnp.zeros_like(acc)
    l_s[...] = jnp.zeros_like(l_s)
    m_s[...] = jnp.full_like(m_s, -1e30)
    hw_copy.wait()
    w_t = w_h[...].astype(jnp.float32).T.astype(jnp.bfloat16)

    def chunk_of(buffer, g):
        return buffer.at[pl.ds(pl.multiple_of(g * PER_CHUNK, PER_CHUNK), PER_CHUNK)]

    def forward(g):
        return pltpu.make_async_remote_copy(
            src_ref=chunk_of(kvbuf, g),
            dst_ref=chunk_of(sibbuf, g),
            send_sem=ssf.at[g],
            recv_sem=rf.at[g],
            device_id=sibling,
            device_id_type=MESH,
        )

    def arrived(buffer, sem):
        pltpu.make_async_copy(buffer, buffer, sem).wait()

    def pass_on(g):
        arrived(chunk_of(kvbuf, g), rkv.at[g])
        forward(g).start()

    def score(g, j, dst):
        q = qbuf[pl.ds(j * PER_CHUNK, PER_CHUNK)].reshape(QB, HEAD_DIM)
        for n, buffer in enumerate((kvbuf, sibbuf)):
            keys = buffer[pl.ds(g * PER_CHUNK, PER_CHUNK), 0].reshape(KC, HEAD_DIM)
            dst[pl.ds(n * KC, KC), :] = lax.dot_general(keys, q, NT, preferred_element_type=jnp.float32)

    def update(j, src, v_t):
        s = src[...]
        m_old = m_s[j]
        m_new = jnp.maximum(m_old, jnp.max(s, axis=0, keepdims=True))
        m_s[j] = m_new
        alpha = jnp.exp2(m_old - m_new)
        e = jnp.exp2(s - m_new[:1])
        l_s[j] = l_s[j] * alpha + jnp.sum(e.reshape(2 * KC // 8, 8, QB), axis=0)
        acc[j] = acc[j] * alpha[:1] + jnp.dot(v_t, e.astype(jnp.bfloat16), preferred_element_type=jnp.float32)

    def give_back(j):
        total = jnp.sum(l_s[j], axis=0, keepdims=True)
        attended = (acc[j] / total).astype(jnp.bfloat16)
        velocity = jnp.dot(w_t, attended, preferred_element_type=jnp.float32).T
        for n in range(PER_CHUNK):
            rows = velocity[n * ROWS : (n + 1) * ROWS]
            i = j * PER_CHUNK + n
            obuf[i] = jnp.concatenate([rows[:HALF], rows[HALF:]], axis=1).astype(jnp.bfloat16)
            pltpu.make_async_remote_copy(
                src_ref=obuf.at[i],
                dst_ref=vbuf.at[i],
                send_sem=sso,
                recv_sem=ro,
                device_id=source(place_before(place, i)),
                device_id_type=MESH,
            ).start()

    arrived(qbuf, rq)
    pass_on(0)

    def chunk(g, _):
        arrived(chunk_of(sibbuf, g), rf.at[g])
        v_t = jnp.concatenate(
            [buffer[pl.ds(g * PER_CHUNK, PER_CHUNK), 1].reshape(KC, HEAD_DIM).T for buffer in (kvbuf, sibbuf)], axis=1
        )
        last = g == CHUNKS - 1
        score(g, 0, s_a)

        def pair(i, _):
            @pl.when(jnp.logical_and(i == N_QB // 2 - 1, jnp.logical_not(last)))
            def _():
                pass_on(g + 1)

            score(g, 2 * i + 1, s_b)
            update(2 * i, s_a, v_t)
            score(g, lax.rem(2 * i + 2, N_QB), s_a)
            update(2 * i + 1, s_b, v_t)

            @pl.when(last)
            def _():
                give_back(2 * i)
                give_back(2 * i + 1)

            return 0

        lax.fori_loop(0, N_QB // 2, pair, 0)
        return 0

    lax.fori_loop(0, CHUNKS, chunk, 0)

    arrived(vbuf, ro)
    velocity = jnp.sum(vbuf[...].astype(jnp.float32), axis=0)
    first = noisy_ref[pl.ds(0, HALF), :] + velocity[:, :64]
    second = noisy_ref[pl.ds(HALF, HALF), :] + velocity[:, 64:]
    lat_ref[pl.ds(0, HALF), :] = first
    lat_ref[pl.ds(HALF, HALF), :] = second
    patches = jnp.concatenate([first, second], axis=1).astype(jnp.bfloat16)
    xsrc[...] = patches
    xrecv[SEC + sec] = patches
    for d in (-1, 0, 1):
        for s in range(1, SEC) if d == 0 else range(SEC):
            pltpu.make_async_remote_copy(
                src_ref=xsrc,
                dst_ref=xrecv.at[(1 - d) * SEC + sec],
                send_sem=ssx,
                recv_sem=rx,
                device_id=(lax.rem(sec + s, SEC), beside(d)),
                device_id_type=MESH,
            ).start()
    arrived(xrecv.at[pl.ds(0, 3 * SEC - 1)], rx)

    for d in range(3):
        got = xrecv[pl.ds(d * SEC, SEC)].reshape(SEC * HALF, 128)
        shifted = [jnp.dot(rowsel_ref[k], got, preferred_element_type=jnp.float32).astype(jnp.bfloat16) for k in range(3)]
        rows = jnp.dot(jnp.concatenate(shifted, axis=1), lanesel_ref[...], preferred_element_type=jnp.float32)
        if d == 0:
            rows = jnp.where(p == 0, 0.0, rows)
        if d == 2:
            rows = jnp.where(p == SEQ - 1, 0.0, rows)
        rows = rows.astype(jnp.bfloat16)
        for f in range(8):
            xf[4 + f, d] = rows[f % 4 * RC : (f % 4 + 1) * RC, f // 4 * 128 : (f // 4 + 1) * 128]
    for l in range(2):
        for f in range(4):
            for a in range(3):
                for n in range(2):
                    lhs[pl.ds((l * 4 + f) * RC, RC), pl.ds(a * 256 + n * 128, 128)] = xf[2 * sec + f + a, l + n]
    row = lax.broadcasted_iota(jnp.int32, (RC, CH), 0)
    is_first = functools.reduce(jnp.logical_or, [row == r * PCOLS for r in range(SEC)])
    is_last = functools.reduce(jnp.logical_or, [row == r * PCOLS + PCOLS - 1 for r in range(SEC)])
    for i in range(2):
        for j in range(2):
            cols = pl.ds((i * 2 + j) * CH, CH)
            hid[:, cols] = jnp.dot(lhs[...], wbig[:, cols], preferred_element_type=jnp.float32) + bias_ref[...]

        def activate(lf, _):
            l, f = lax.div(lf, 4), lax.rem(lf, 4)
            y = 2 * l + i
            outside = jnp.logical_or(jnp.logical_and(sec == 0, f < 2), jnp.logical_or(jnp.logical_and(p == 0, y == 0), jnp.logical_and(p == SEQ - 1, y == 3)))
            for j in range(2):
                x = hid[pl.ds(pl.multiple_of(lf * RC, RC), RC), pl.ds((i * 2 + j) * CH, CH)].astype(jnp.bfloat16).astype(jnp.float32)
                x = x * lax.rsqrt(jnp.mean(x * x, axis=-1, keepdims=True) + EPS) * vg_ref[...]
                x = jnp.where(outside, 0.0, x / (1.0 + jnp.exp(-x)))
                tap[f, y, :, pl.ds((1 + j) * CH, CH)] = x.astype(jnp.bfloat16)
                if j == 0:
                    x = jnp.where(is_last, 0.0, pltpu.roll(x, RC - 1, 0))
                    tap[f, y, :, pl.ds(3 * CH, CH)] = x.astype(jnp.bfloat16)
                else:
                    x = jnp.where(is_first, 0.0, pltpu.roll(x, 1, 0))
                    tap[f, y, :, pl.ds(0, CH)] = x.astype(jnp.bfloat16)
            return 0

        lax.fori_loop(0, 8, activate, 0)

    w_copy.wait()
    cacc[...] = jnp.zeros_like(cacc)

    def one_tap(t, _):
        a, b = lax.div(t, 3), lax.rem(t, 3)
        block = tap[pl.ds(a, 2), pl.ds(b, 2)].reshape(4 * RC, 4 * CH)
        both = jnp.concatenate([block[:, : 3 * CH], block[:, CH:]], axis=0)
        cacc[...] += jnp.dot(both, wconv[t], preferred_element_type=jnp.float32)
        return 0

    lax.fori_loop(0, 9, one_tap, 0)
    for f in range(2):
        for y in range(2):
            rows = pl.ds((y * 4 + 2 + f) * RC, RC)
            for j in range(2):
                hidden = hid[rows, pl.ds(((1 - y) * 2 + j) * CH, CH)].astype(jnp.bfloat16).astype(jnp.float32)
                out = hidden + cacc[pl.ds(((j * 2 + f) * 2 + y) * RC, RC), :]
                dec_ref[f, y, :, pl.ds(j * CH, CH)] = out.astype(jnp.bfloat16)

    arrived(qsrc, ssq)
    arrived(kvsrc, sskv)
    arrived(obuf, sso)
    arrived(xrecv.at[pl.ds(0, 3 * SEC - 1)], ssx)

    def sent(g, _):
        arrived(chunk_of(kvbuf, g), ssf.at[g])
        return 0

    lax.fori_loop(0, CHUNKS, sent, 0)


def shards(
    queries, keys, values, query_gain, key_gain, noisy, head_weight, conv_in_weight, conv_in_bias, vae_gain, conv_weight
):
    rowsel, lanesel = gather_constants()
    vmem = pl.BlockSpec(memory_space=pltpu.VMEM)
    anywhere = pl.BlockSpec(memory_space=pl.ANY)
    bf16, f32, dma = jnp.bfloat16, jnp.float32, pltpu.SemaphoreType.DMA
    latents, decoded = pl.pallas_call(
        kernel,
        out_shape=(jax.ShapeDtypeStruct((ROWS, 64), f32), jax.ShapeDtypeStruct((2, 2, RC, 2 * CH), bf16)),
        in_specs=[vmem] * 6 + [anywhere] + [vmem] * 3 + [anywhere] + [vmem] * 2,
        out_specs=(vmem, vmem),
        scratch_shapes=[
            pltpu.VMEM((HEADS, ROWS, HEAD_DIM), bf16),
            pltpu.VMEM((HEADS, 2, ROWS, HEAD_DIM), bf16),
            pltpu.VMEM((STEPS, ROWS, HEAD_DIM), bf16),
            pltpu.VMEM((STEPS, 2, ROWS, HEAD_DIM), bf16),
            pltpu.VMEM((STEPS, 2, ROWS, HEAD_DIM), bf16),
            pltpu.VMEM((N_QB, HEAD_DIM, QB), f32),
            pltpu.VMEM((N_QB, 8, QB), f32),
            pltpu.VMEM((N_QB, 8, QB), f32),
            pltpu.VMEM((2 * KC, QB), f32),
            pltpu.VMEM((2 * KC, QB), f32),
            pltpu.VMEM((STEPS, HALF, 128), bf16),
            pltpu.VMEM((STEPS, HALF, 128), bf16),
            pltpu.VMEM((HALF, 128), bf16),
            pltpu.VMEM((3 * SEC, HALF, 128), bf16),
            pltpu.VMEM((12, 3, RC, 128), bf16),
            pltpu.VMEM((8 * RC, 768), bf16),
            pltpu.VMEM((8 * RC, 4 * CH), f32),
            pltpu.VMEM((4, 4, RC, 4 * CH), bf16),
            pltpu.VMEM((768, 4 * CH), bf16),
            pltpu.VMEM((9, 3 * CH, CH), bf16),
            pltpu.VMEM((HEAD_DIM, 64), bf16),
            pltpu.VMEM((8 * RC, CH), f32),
            dma, dma, dma((CHUNKS,)), dma, dma, dma, dma((CHUNKS,)), dma((CHUNKS,)), dma, dma, dma((2,)),
        ],
        compiler_params=pltpu.CompilerParams(collective_id=0, has_side_effects=True, vmem_limit_bytes=56 * 2**20),
        name="step",
    )(
        queries[0],
        keys[0],
        values[0],
        query_gain.reshape(1, -1),
        key_gain.reshape(1, -1),
        noisy[0],
        head_weight,
        conv_in_weight.reshape(432, CH),
        conv_in_bias.reshape(1, CH),
        vae_gain.reshape(1, CH),
        conv_weight.reshape(9, 3 * CH, CH),
        jnp.asarray(rowsel, bf16),
        jnp.asarray(lanesel, bf16),
    )
    decoded = decoded.reshape(2, 2, SEC, PCOLS, 2, CH).transpose(2, 0, 1, 3, 4, 5)
    return latents[None], decoded.reshape(SEC, 2, 2, 2 * PCOLS, CH)


def solution(mesh):
    placed = (
        P("sec", "seq", None),
        P("sec", "seq", None),
        P("sec", "seq", None),
        P(),
        P(),
        P("sec", "seq", None),
        P(),
        P(),
        P(),
        P(),
        P(),
    )
    return jax.shard_map(
        shards,
        mesh=mesh,
        in_specs=placed,
        out_specs=(P("sec", "seq", None), P(None, "sec", "seq", None, None)),
        check_vma=False,
    )
```

```python
import functools
import math

import jax
import jax.numpy as jnp
import numpy as np
from jax import lax
from jax.experimental import pallas as pl
from jax.experimental.pallas import tpu as pltpu
from jax.sharding import PartitionSpec as P

HEADS = 32
HEAD_DIM = 128
ROWS = 96
HALF = ROWS // 2
SEQ = 64
SEC = 4
STEPS = 32
PER_CHUNK = 4
CHUNKS = STEPS // PER_CHUNK
AHEAD = 2
PER_QB = 8
QB = PER_QB * ROWS
N_QB = STEPS // PER_QB
KC = 2 * PER_CHUNK * ROWS
KV_ROWS = ROWS + HALF
PCOLS = 12
RC = SEC * PCOLS
CH = 384
EPS = 1e-06
MESH = pl.DeviceIdType.MESH
NT = (((1,), (1,)), ((), ()))
LOG2E = 1.0 / math.log(2.0)


def offsets(i):
    b, c = i // 4, i % 4
    return (b // 4 + c // 2) % 2, (b + c) % 4, c


def gather_constants():
    rows = np.zeros((3, 4 * RC, 4 * RC), np.float32)
    lanes = np.zeros((3, 128, 256), np.float32)
    for k in range(3):
        for f in range(4):
            for r in range(SEC):
                for c in range(PCOLS):
                    if 0 <= c + k - 1 < PCOLS:
                        rows[k, (f * SEC + r) * PCOLS + c, (r * 4 + f) * PCOLS + c + k - 1] = 1
    for half in range(2):
        for i in range(2):
            for tap, (k, j) in enumerate(((0, 1), (1, 0), (1, 1), (2, 0))):
                for ch in range(16):
                    lanes[k, half * 64 + i * 32 + j * 16 + ch, half * 128 + i * 64 + tap * 16 + ch] = 1
    return rows, lanes.reshape(384, 256)


def kernel(
    q_hbm, k_hbm, v_hbm, qg_ref, kg_ref, noisy_ref, hw_ref, win_ref, bias_ref, vg_ref, w_ref, rowsel_ref, lanesel_ref,
    lat_ref, dec_ref,
    q_ref, k_ref, v_ref, qsrc, kvsrc, qbuf, kvbuf, sibbuf, keys, values, acc, m_s, l_s, s_a, s_b, obuf, vbuf,
    noisy_s, xsrc, xrecv, xf, lhs, hid, tap, wbig, wconv, cacc, dec_s,
    ssq, sskv, ssf, sso, ssx, rq, rkv, rf, ro, rx, lsem,
):
    sec, p = lax.axis_index("sec"), lax.axis_index("seq")
    z_lo, core = lax.div(sec, 2), lax.rem(sec, 2)
    part, place = lax.div(p, 32), lax.rem(p, 32)
    local = [
        pltpu.make_async_copy(src, dst, lsem.at[n])
        for n, (src, dst) in enumerate(((q_hbm, q_ref), (k_hbm, k_ref), (v_hbm, v_ref), (w_ref, wconv)))
    ]
    for copy in local:
        copy.start()

    place_y, place_x, place_z = lax.div(place, 16), lax.rem(lax.div(place, 4), 4), lax.rem(place, 4)
    ys = [lax.rem(place_y + n, 2) * 16 for n in range(2)]
    xs = [lax.rem(place_x + n, 4) * 4 for n in range(4)]
    zs = [lax.rem(place_z + n, 4) for n in range(4)]

    def target(h):
        return (2 * z_lo + 1 - part, h + 32 * core)

    def source(j):
        return (2 * z_lo + part, j + 32 * (1 - core))

    def head_at(i):
        dy, dx, dz = offsets(i)
        return ys[dy] + xs[dx] + zs[dz]

    def source_at(i):
        dy, dx, dz = offsets(i)
        return source(ys[dy] + xs[-dx % 4] + zs[-dz % 4])

    sibling = (2 * z_lo + 1 - core, p)

    def beside(d):
        return lax.rem(p + SEQ + d, SEQ)

    barrier = pltpu.get_barrier_semaphore()
    for i in range(STEPS):
        pl.semaphore_signal(barrier, inc=1, device_id=target(head_at(i)), device_id_type=MESH)
        pl.semaphore_signal(barrier, inc=1, device_id=source_at(i), device_id_type=MESH)
    pl.semaphore_signal(barrier, inc=1, device_id=sibling, device_id_type=MESH)
    for d in (-1, 0, 1):
        for s in range(1, SEC) if d == 0 else range(SEC):
            pl.semaphore_signal(barrier, inc=1, device_id=(lax.rem(sec + s, SEC), beside(d)), device_id_type=MESH)

    def normed(ref, gain_ref, factor, store):
        def some(t, _):
            rows = pl.ds(pl.multiple_of(t * 16, 16), 16)
            x = ref[rows, :].astype(jnp.float32)
            scale = lax.rsqrt(jnp.mean(x * x, axis=-1, keepdims=True) + EPS)
            for h in range(HEADS):
                cols = slice(h * HEAD_DIM, (h + 1) * HEAD_DIM)
                y = x[:, cols] * scale * gain_ref[:, cols]
                store(h, rows, (y if factor is None else y * factor).astype(jnp.bfloat16))
            return 0

        lax.fori_loop(0, ROWS // 16, some, 0)

    def store_q(h, rows, y):
        qsrc[h, rows, :] = y

    def store_k(h, rows, y):
        kvsrc[h, rows, :] = y

    local[0].wait()
    normed(q_ref, qg_ref, LOG2E / math.sqrt(HEAD_DIM), store_q)
    pl.semaphore_wait(barrier, 2 * STEPS + 1 + 3 * SEC - 1)
    for i in range(STEPS):
        h = head_at(i)
        pltpu.make_async_remote_copy(
            src_ref=qsrc.at[h], dst_ref=qbuf.at[i], send_sem=ssq, recv_sem=rq, device_id=target(h), device_id_type=MESH
        ).start()
    local[1].wait()
    normed(k_ref, kg_ref, None, store_k)
    local[2].wait()
    for h in range(HEADS):
        cols = slice(h * HEAD_DIM, (h + 1) * HEAD_DIM)
        weighted = lax.dot_general(v_ref[:, cols], hw_ref[:, cols], NT, preferred_element_type=jnp.float32)
        kvsrc[h, pl.ds(ROWS, HALF)] = jnp.concatenate([weighted[:HALF], weighted[HALF:]], axis=1).astype(jnp.bfloat16)

    def send_chunk(g):
        for n in range(PER_CHUNK):
            y = lax.rem(place_y + lax.div(g, 4) + n // 2, 2)
            x = lax.rem(place_x + g + n, 4)
            h = y * 16 + x * 4 + zs[n]
            pltpu.make_async_remote_copy(
                src_ref=kvsrc.at[h],
                dst_ref=kvbuf.at[g * PER_CHUNK + n],
                send_sem=sskv,
                recv_sem=rkv.at[g],
                device_id=target(h),
                device_id_type=MESH,
            ).start()

    def arrived(buffer, sem):
        pltpu.make_async_copy(buffer, buffer, sem).wait()

    send_chunk(0)
    wbig[...] = jnp.zeros_like(wbig)
    for a in range(3):
        for b in range(3):
            block = win_ref[pl.ds((a * 3 + b) * 48, 48), :]
            for i in range(2):
                for j in range(2):
                    wbig[pl.ds(a * 256 + (b + i) * 64 + j * 16, 48), pl.ds((i * 2 + j) * CH, CH)] = block
    xf[pl.ds(0, 4)] = jnp.zeros((4,) + xf.shape[1:], jnp.bfloat16)
    noisy = noisy_ref[...].T
    noisy_s[...] = jnp.concatenate([noisy[:HALF], noisy[HALF:]], axis=1)
    acc[...] = jnp.zeros_like(acc)
    l_s[...] = jnp.zeros_like(l_s)
    m_s[...] = jnp.full_like(m_s, -1e30)
    arrived(qsrc, ssq)
    for g in range(1, AHEAD):
        send_chunk(g)

    def chunk_of(buffer, g):
        return buffer.at[pl.ds(g * PER_CHUNK, PER_CHUNK)]

    def pass_on(g):
        arrived(chunk_of(kvbuf, g), rkv.at[g])
        pltpu.make_async_remote_copy(
            src_ref=chunk_of(kvbuf, g),
            dst_ref=chunk_of(sibbuf, g),
            send_sem=ssf.at[g],
            recv_sem=rf.at[g],
            device_id=sibling,
            device_id_type=MESH,
        ).start()

    def take(g):
        arrived(chunk_of(sibbuf, g), rf.at[g])
        steps = pl.ds(g * PER_CHUNK, PER_CHUNK)
        for half in range(2):
            for n, buffer in enumerate((kvbuf, sibbuf)):
                keys[pl.ds((half * 2 + n) * KC // 4, KC // 4), :] = buffer[steps, pl.ds(half * HALF, HALF)].reshape(KC // 4, HEAD_DIM)
        both = jnp.concatenate([buffer[steps, pl.ds(ROWS, HALF)].reshape(KC // 4, 128) for buffer in (kvbuf, sibbuf)], axis=0).T
        values[:, pl.ds(0, KC // 2)] = both[:64]
        values[:, pl.ds(KC // 2, KC // 2)] = both[64:]

    def score(j, dst):
        q = qbuf[pl.ds(j * PER_QB, PER_QB)].reshape(QB, HEAD_DIM)
        dst[...] = lax.dot_general(keys[...], q, NT, preferred_element_type=jnp.float32)

    def update(j, src):
        s = src[...]
        m_old = m_s[j]
        m_new = jnp.maximum(m_old, jnp.max(s, axis=0, keepdims=True))
        m_s[j] = m_new
        alpha = jnp.exp2(m_old - m_new)
        e = jnp.exp2(s - m_new[:1])
        l_s[j] = l_s[j] * alpha + jnp.sum(e.reshape(KC // 8, 8, QB), axis=0)
        acc[j] = acc[j] * alpha[:1] + jnp.dot(values[...], e.astype(jnp.bfloat16), preferred_element_type=jnp.float32)

    def give_back(j):
        total = jnp.sum(l_s[j], axis=0, keepdims=True)
        velocity = (acc[j] * (1.0 / total)).T
        for n in range(PER_QB):
            rows = velocity[n * ROWS : (n + 1) * ROWS]
            i = j * PER_QB + n
            obuf[i] = jnp.concatenate([rows[:HALF], rows[HALF:]], axis=1).astype(jnp.bfloat16)
            pltpu.make_async_remote_copy(
                src_ref=obuf.at[i],
                dst_ref=vbuf.at[i],
                send_sem=sso,
                recv_sem=ro,
                device_id=source_at(i),
                device_id_type=MESH,
            ).start()

    arrived(qbuf, rq)
    pass_on(0)

    def chunk(g, _):
        take(g)

        @pl.when(g + AHEAD < CHUNKS)
        def _():
            send_chunk(g + AHEAD)

        last = g == CHUNKS - 1
        score(0, s_a)
        for i in range(N_QB // 2):
            if i == N_QB // 2 - 1:
                pl.when(jnp.logical_not(last))(lambda: pass_on(g + 1))
            score(2 * i + 1, s_b)
            update(2 * i, s_a)
            pl.when(last)(lambda: give_back(2 * i))
            if i < N_QB // 2 - 1:
                score(2 * i + 2, s_a)
            update(2 * i + 1, s_b)
            pl.when(last)(lambda: give_back(2 * i + 1))
        return 0

    lax.fori_loop(0, CHUNKS, chunk, 0)

    arrived(vbuf, ro)
    latents = noisy_s[...] + jnp.sum(vbuf[...].astype(jnp.float32), axis=0)
    patches = latents.astype(jnp.bfloat16)
    xsrc[...] = patches
    xrecv[SEC + sec] = patches
    for d in (-1, 0, 1):
        for s in range(1, SEC) if d == 0 else range(SEC):
            pltpu.make_async_remote_copy(
                src_ref=xsrc,
                dst_ref=xrecv.at[(1 - d) * SEC + sec],
                send_sem=ssx,
                recv_sem=rx,
                device_id=(lax.rem(sec + s, SEC), beside(d)),
                device_id_type=MESH,
            ).start()
    lat_ref[...] = jnp.concatenate([latents[:, :64], latents[:, 64:]], axis=0).T
    arrived(xrecv.at[pl.ds(0, 3 * SEC - 1)], rx)

    for d in range(3):
        got = xrecv[pl.ds(d * SEC, SEC)].reshape(SEC * HALF, 128)
        shifted = [jnp.dot(rowsel_ref[k], got, preferred_element_type=jnp.float32).astype(jnp.bfloat16) for k in range(3)]
        rows = jnp.dot(jnp.concatenate(shifted, axis=1), lanesel_ref[...], preferred_element_type=jnp.float32)
        if d == 0:
            rows = jnp.where(p == 0, 0.0, rows)
        if d == 2:
            rows = jnp.where(p == SEQ - 1, 0.0, rows)
        rows = rows.astype(jnp.bfloat16)
        for f in range(8):
            xf[4 + f, d] = rows[f % 4 * RC : (f % 4 + 1) * RC, f // 4 * 128 : (f // 4 + 1) * 128]
    for l in range(2):
        for f in range(4):
            for a in range(3):
                for n in range(2):
                    lhs[pl.ds((l * 4 + f) * RC, RC), pl.ds(a * 256 + n * 128, 128)] = xf[2 * sec + f + a, l + n]
    row = lax.broadcasted_iota(jnp.int32, (RC, CH), 0)
    is_first = functools.reduce(jnp.logical_or, [row == r * PCOLS for r in range(SEC)])
    is_last = functools.reduce(jnp.logical_or, [row == r * PCOLS + PCOLS - 1 for r in range(SEC)])
    bias, gain = bias_ref[...].reshape(1, CH), vg_ref[...].reshape(1, CH)

    def convolve(n):
        cols = pl.ds(n * CH, CH)
        hid[:, cols] = jnp.dot(lhs[...], wbig[:, cols], preferred_element_type=jnp.float32) + bias

    def activate(n):
        i, j = n // 2, n % 2
        for l in range(2):
            for f in range(4):
                y = 2 * l + i
                x = hid[pl.ds((l * 4 + f) * RC, RC), pl.ds(n * CH, CH)].astype(jnp.bfloat16).astype(jnp.float32)
                x = x * lax.rsqrt(jnp.mean(x * x, axis=-1, keepdims=True) + EPS) * gain
                x = 0.5 * x
                x = x + x * jnp.tanh(x)
                outside = [sec == 0] * (f < 2) + [p == 0] * (y == 0) + [p == SEQ - 1] * (y == 3)
                if outside:
                    x = jnp.where(functools.reduce(jnp.logical_or, outside), 0.0, x)
                tap[f, y, :, pl.ds((1 + j) * CH, CH)] = x.astype(jnp.bfloat16)
                if j == 0:
                    x = jnp.where(is_last, 0.0, pltpu.roll(x, RC - 1, 0))
                    tap[f, y, :, pl.ds(3 * CH, CH)] = x.astype(jnp.bfloat16)
                else:
                    x = jnp.where(is_first, 0.0, pltpu.roll(x, 1, 0))
                    tap[f, y, :, pl.ds(0, CH)] = x.astype(jnp.bfloat16)

    convolve(0)
    for n in range(4):
        if n < 3:
            convolve(n + 1)
        activate(n)

    local[3].wait()
    cacc[...] = jnp.zeros_like(cacc)

    def one_tap(t, _):
        a, b = lax.div(t, 3), lax.rem(t, 3)
        block = tap[pl.ds(a, 2), pl.ds(b, 2)].reshape(4 * RC, 4 * CH)
        both = jnp.concatenate([block[:, : 3 * CH], block[:, CH:]], axis=0)
        cacc[...] += jnp.dot(both, wconv[t], preferred_element_type=jnp.float32)
        return 0

    lax.fori_loop(0, 9, one_tap, 0)
    for f in range(2):
        for y in range(2):
            rows = pl.ds((y * 4 + 2 + f) * RC, RC)
            for j in range(2):
                hidden = hid[rows, pl.ds(((1 - y) * 2 + j) * CH, CH)].astype(jnp.bfloat16).astype(jnp.float32)
                out = hidden + cacc[pl.ds(((j * 2 + f) * 2 + y) * RC, RC), :]
                for r in range(SEC):
                    for n in range(CH // 128):
                        part_out = out[r * PCOLS : (r + 1) * PCOLS, n * 128 : (n + 1) * 128]
                        dec_s[r, f, y, n, pl.ds(j, PCOLS, 2), :] = part_out
            for r in range(SEC):
                for n in range(CH // 128):
                    dec_ref[r, f, y, :, pl.ds(n * 128, 128)] = dec_s[r, f, y, n].astype(jnp.bfloat16)

    arrived(kvsrc, sskv)
    arrived(obuf, sso)
    arrived(xrecv.at[pl.ds(0, 3 * SEC - 1)], ssx)

    def sent(g, _):
        arrived(chunk_of(kvbuf, g), ssf.at[g])
        return 0

    lax.fori_loop(0, CHUNKS, sent, 0)


def shards(
    queries, keys, values, query_gain, key_gain, noisy, head_weight, conv_in_weight, conv_in_bias, vae_gain, conv_weight
):
    rowsel, lanesel = gather_constants()
    vmem = pl.BlockSpec(memory_space=pltpu.VMEM)
    anywhere = pl.BlockSpec(memory_space=pl.ANY)
    bf16, f32, dma = jnp.bfloat16, jnp.float32, pltpu.SemaphoreType.DMA
    latents, decoded = pl.pallas_call(
        kernel,
        out_shape=(jax.ShapeDtypeStruct((64, ROWS), f32), jax.ShapeDtypeStruct((SEC, 2, 2, 2 * PCOLS, CH), bf16)),
        in_specs=[anywhere] * 3 + [vmem] * 7 + [anywhere] + [vmem] * 2,
        out_specs=(vmem, vmem),
        scratch_shapes=[
            *[pltpu.VMEM((ROWS, HEADS * HEAD_DIM), bf16)] * 3,
            pltpu.VMEM((HEADS, ROWS, HEAD_DIM), bf16),
            pltpu.VMEM((HEADS, KV_ROWS, HEAD_DIM), bf16),
            pltpu.VMEM((STEPS, ROWS, HEAD_DIM), bf16),
            pltpu.VMEM((STEPS, KV_ROWS, HEAD_DIM), bf16),
            pltpu.VMEM((STEPS, KV_ROWS, HEAD_DIM), bf16),
            pltpu.VMEM((KC, HEAD_DIM), bf16),
            pltpu.VMEM((64, KC), bf16),
            pltpu.VMEM((N_QB, 64, QB), f32),
            pltpu.VMEM((N_QB, 8, QB), f32),
            pltpu.VMEM((N_QB, 8, QB), f32),
            pltpu.VMEM((KC, QB), f32),
            pltpu.VMEM((KC, QB), f32),
            pltpu.VMEM((STEPS, HALF, 128), bf16),
            pltpu.VMEM((STEPS, HALF, 128), bf16),
            pltpu.VMEM((HALF, 128), f32),
            pltpu.VMEM((HALF, 128), bf16),
            pltpu.VMEM((3 * SEC, HALF, 128), bf16),
            pltpu.VMEM((12, 3, RC, 128), bf16),
            pltpu.VMEM((8 * RC, 768), bf16),
            pltpu.VMEM((8 * RC, 4 * CH), f32),
            pltpu.VMEM((4, 4, RC, 4 * CH), bf16),
            pltpu.VMEM((768, 4 * CH), bf16),
            pltpu.VMEM((9, 3 * CH, CH), bf16),
            pltpu.VMEM((8 * RC, CH), f32),
            pltpu.VMEM((SEC, 2, 2, CH // 128, 2 * PCOLS, 128), f32),
            dma, dma, dma((CHUNKS,)), dma, dma, dma, dma((CHUNKS,)), dma((CHUNKS,)), dma, dma, dma((4,)),
        ],
        compiler_params=pltpu.CompilerParams(collective_id=0, has_side_effects=True, vmem_limit_bytes=56 * 2**20),
        name="step",
    )(
        queries[0],
        keys[0],
        values[0],
        query_gain.reshape(1, -1),
        key_gain.reshape(1, -1),
        noisy[0].T,
        head_weight.T,
        conv_in_weight.reshape(432, CH),
        conv_in_bias,
        vae_gain,
        conv_weight.reshape(9, 3 * CH, CH),
        jnp.asarray(rowsel, bf16),
        jnp.asarray(lanesel, bf16),
    )
    return latents.T[None], decoded


def solution(mesh):
    placed = (
        P("sec", "seq", None),
        P("sec", "seq", None),
        P("sec", "seq", None),
        P(),
        P(),
        P("sec", "seq", None),
        P(),
        P(),
        P(),
        P(),
        P(),
    )
    return jax.shard_map(
        shards,
        mesh=mesh,
        in_specs=placed,
        out_specs=(P("sec", "seq", None), P(None, "sec", "seq", None, None)),
        check_vma=False,
    )
```

```python
import functools
import math

import jax
import jax.numpy as jnp
import numpy as np
from jax import lax
from jax.experimental import pallas as pl
from jax.experimental.pallas import tpu as pltpu
from jax.sharding import PartitionSpec as P

HEADS = 32
HEAD_DIM = 128
ROWS = 96
HALF = ROWS // 2
SEQ = 64
SEC = 4
STEPS = 32
PER_CHUNK = 4
CHUNKS = STEPS // PER_CHUNK
AHEAD = 3
PER_QB = 8
QB = PER_QB * ROWS
N_QB = STEPS // PER_QB
PEERS = STEPS // 4
KC = 2 * PER_CHUNK * ROWS
KV_ROWS = ROWS + HALF
PCOLS = 12
RC = SEC * PCOLS
CH = 384
EPS = 1e-06
MESH = pl.DeviceIdType.MESH
NT = (((1,), (1,)), ((), ()))
LOG2E = 1.0 / math.log(2.0)


def offsets(i):
    b, c = i // 4, i % 4
    return (b // 4 + c // 2) % 2, (b + c) % 4, c


def gather_constants():
    rows = np.zeros((3, 4 * RC, 4 * RC), np.float32)
    lanes = np.zeros((3, 128, 256), np.float32)
    for k in range(3):
        for f in range(4):
            for r in range(SEC):
                for c in range(PCOLS):
                    if 0 <= c + k - 1 < PCOLS:
                        rows[k, (f * SEC + r) * PCOLS + c, (r * 4 + f) * PCOLS + c + k - 1] = 1
    for half in range(2):
        for i in range(2):
            for tap, (k, j) in enumerate(((0, 1), (1, 0), (1, 1), (2, 0))):
                for ch in range(16):
                    lanes[k, half * 64 + i * 32 + j * 16 + ch, half * 128 + i * 64 + tap * 16 + ch] = 1
    return rows, lanes.reshape(384, 256)


def kernel(
    q_hbm, k_hbm, v_hbm, qg_ref, kg_ref, noisy_ref, hw_ref, win_ref, bias_ref, vg_ref, w_ref, rowsel_ref, lanesel_ref,
    lat_ref, dec_ref,
    q_ref, k_ref, v_ref, qsrc, kvsrc, qbuf, kvbuf, sibbuf, keys, values, acc, m_s, l_s, s_a, s_b, gsrc, gbuf, hsrc, vbuf,
    noisy_s, xsrc, xrecv, xf, lhs, hid, tap, wbig, wconv, cacc, dec_s,
    ssq, sskv, ssf, sso, ssh, ssx, rq, rkv, rf, ro, rh, rx, lsem,
):
    sec, p = lax.axis_index("sec"), lax.axis_index("seq")
    z_lo, core = lax.div(sec, 2), lax.rem(sec, 2)
    part, place = lax.div(p, 32), lax.rem(p, 32)
    local = [
        pltpu.make_async_copy(src, dst, lsem.at[n])
        for n, (src, dst) in enumerate(((q_hbm, q_ref), (k_hbm, k_ref), (v_hbm, v_ref), (w_ref, wconv)))
    ]
    for copy in local[:3]:
        copy.start()

    place_y, place_x, place_z = lax.div(place, 16), lax.rem(lax.div(place, 4), 4), lax.rem(place, 4)
    ys = [lax.rem(place_y + n, 2) * 16 for n in range(2)]
    xs = [lax.rem(place_x + n, 4) * 4 for n in range(4)]
    zs = [lax.rem(place_z + n, 4) for n in range(4)]

    def target(h):
        return (2 * z_lo + 1 - part, h + 32 * core)

    def source(j):
        return (2 * z_lo + part, j + 32 * (1 - core))

    def head_at(i):
        dy, dx, dz = offsets(i)
        return ys[dy] + xs[dx] + zs[dz]

    def source_at(i):
        dy, dx, dz = offsets(i)
        return source(ys[dy] + xs[-dx % 4] + zs[-dz % 4])

    def peer_at(e):
        return (sec, ys[e // 4] + xs[-e % 4] + place_z + 32 * part)

    sibling = (2 * z_lo + 1 - core, p)

    def beside(d):
        return lax.rem(p + SEQ + d, SEQ)

    barrier = pltpu.get_barrier_semaphore()
    for i in range(STEPS):
        pl.semaphore_signal(barrier, inc=1, device_id=target(head_at(i)), device_id_type=MESH)
        pl.semaphore_signal(barrier, inc=1, device_id=source_at(i), device_id_type=MESH)
    pl.semaphore_signal(barrier, inc=1, device_id=sibling, device_id_type=MESH)
    for e in range(1, PEERS):
        pl.semaphore_signal(barrier, inc=1, device_id=peer_at(e), device_id_type=MESH)
    for d in (-1, 0, 1):
        for s in range(1, SEC) if d == 0 else range(SEC):
            pl.semaphore_signal(barrier, inc=1, device_id=(lax.rem(sec + s, SEC), beside(d)), device_id_type=MESH)

    def normed(ref, gain_ref, factor, store):
        def some(t, _):
            rows = pl.ds(pl.multiple_of(t * 16, 16), 16)
            x = ref[rows, :].astype(jnp.float32)
            scale = lax.rsqrt(jnp.mean(x * x, axis=-1, keepdims=True) + EPS)
            for h in range(HEADS):
                cols = slice(h * HEAD_DIM, (h + 1) * HEAD_DIM)
                y = x[:, cols] * scale * gain_ref[:, cols]
                store(h, rows, (y if factor is None else y * factor).astype(jnp.bfloat16))
            return 0

        lax.fori_loop(0, ROWS // 16, some, 0)

    def store_q(h, rows, y):
        qsrc[h, rows, :] = y

    def store_k(h, rows, y):
        kvsrc[h, rows, :] = y

    local[0].wait()
    normed(q_ref, qg_ref, LOG2E / math.sqrt(HEAD_DIM), store_q)
    pl.semaphore_wait(barrier, 2 * STEPS + 1 + PEERS - 1 + 3 * SEC - 1)
    for i in range(STEPS):
        h = ys[i // 16] + xs[i // 4 % 4] + zs[i % 4]
        pltpu.make_async_remote_copy(
            src_ref=qsrc.at[h], dst_ref=qbuf.at[i], send_sem=ssq, recv_sem=rq, device_id=target(h), device_id_type=MESH
        ).start()
    local[3].start()
    local[1].wait()
    normed(k_ref, kg_ref, None, store_k)
    local[2].wait()
    for h in range(HEADS):
        cols = slice(h * HEAD_DIM, (h + 1) * HEAD_DIM)
        weighted = lax.dot_general(v_ref[:, cols], hw_ref[:, cols], NT, preferred_element_type=jnp.float32)
        kvsrc[h, pl.ds(ROWS, HALF)] = jnp.concatenate([weighted[:HALF], weighted[HALF:]], axis=1).astype(jnp.bfloat16)

    def send_chunk(g):
        for n in range(PER_CHUNK):
            y = lax.rem(place_y + lax.div(g, 4) + n // 2, 2)
            x = lax.rem(place_x + g + n, 4)
            h = y * 16 + x * 4 + zs[n]
            pltpu.make_async_remote_copy(
                src_ref=kvsrc.at[h],
                dst_ref=kvbuf.at[g * PER_CHUNK + n],
                send_sem=sskv,
                recv_sem=rkv.at[g],
                device_id=target(h),
                device_id_type=MESH,
            ).start()

    def arrived(buffer, sem):
        pltpu.make_async_copy(buffer, buffer, sem).wait()

    send_chunk(0)
    wbig[...] = jnp.zeros_like(wbig)
    for a in range(3):
        for b in range(3):
            block = win_ref[pl.ds((a * 3 + b) * 48, 48), :]
            for i in range(2):
                for j in range(2):
                    wbig[pl.ds(a * 256 + (b + i) * 64 + j * 16, 48), pl.ds((i * 2 + j) * CH, CH)] = block
    xf[pl.ds(0, 4)] = jnp.zeros((4,) + xf.shape[1:], jnp.bfloat16)
    noisy = noisy_ref[...].T
    noisy_s[...] = jnp.concatenate([noisy[:HALF], noisy[HALF:]], axis=1)
    acc[...] = jnp.zeros_like(acc)
    l_s[...] = jnp.zeros_like(l_s)
    m_s[...] = jnp.full_like(m_s, -1e30)
    arrived(qsrc, ssq)
    for g in range(1, AHEAD):
        send_chunk(g)

    def chunk_of(buffer, g):
        return buffer.at[pl.ds(g * PER_CHUNK, PER_CHUNK)]

    def pass_on(g):
        arrived(chunk_of(kvbuf, g), rkv.at[g])
        pltpu.make_async_remote_copy(
            src_ref=chunk_of(kvbuf, g),
            dst_ref=chunk_of(sibbuf, g),
            send_sem=ssf.at[g],
            recv_sem=rf.at[g],
            device_id=sibling,
            device_id_type=MESH,
        ).start()

    def take(g):
        arrived(chunk_of(sibbuf, g), rf.at[g])
        steps = pl.ds(g * PER_CHUNK, PER_CHUNK)
        for half in range(2):
            for n, buffer in enumerate((kvbuf, sibbuf)):
                keys[pl.ds((half * 2 + n) * KC // 4, KC // 4), :] = buffer[steps, pl.ds(half * HALF, HALF)].reshape(KC // 4, HEAD_DIM)
        both = jnp.concatenate([buffer[steps, pl.ds(ROWS, HALF)].reshape(KC // 4, 128) for buffer in (kvbuf, sibbuf)], axis=0).T
        values[:, pl.ds(0, KC // 2)] = both[:64]
        values[:, pl.ds(KC // 2, KC // 2)] = both[64:]

    def score(j, dst):
        q = qbuf[pl.ds(j * PER_QB, PER_QB)].reshape(QB, HEAD_DIM)
        dst[...] = lax.dot_general(keys[...], q, NT, preferred_element_type=jnp.float32)

    def update(j, src):
        s = src[...]
        m_old = m_s[j]
        m_new = jnp.maximum(m_old, jnp.max(s, axis=0, keepdims=True))
        m_s[j] = m_new
        alpha = jnp.exp2(m_old - m_new)
        e = jnp.exp2(s - m_new[:1])
        l_s[j] = l_s[j] * alpha + jnp.sum(e.reshape(KC // 8, 8, QB), axis=0)
        acc[j] = acc[j] * alpha[:1] + jnp.dot(values[...], e.astype(jnp.bfloat16), preferred_element_type=jnp.float32)

    def give_back(j):
        total = jnp.sum(l_s[j], axis=0, keepdims=True)
        velocity = (acc[j] * (1.0 / total)).T
        for e in range(j * PER_QB // 4, (j + 1) * PER_QB // 4):
            to = gbuf if e == 0 else gsrc
            for dz in range(4):
                n = e * 4 + dz - j * PER_QB
                rows = velocity[n * ROWS : (n + 1) * ROWS]
                to[e, dz] = jnp.concatenate([rows[:HALF], rows[HALF:]], axis=1).astype(jnp.bfloat16)
            if e:
                pltpu.make_async_remote_copy(
                    src_ref=gsrc.at[e], dst_ref=gbuf.at[e], send_sem=sso, recv_sem=ro, device_id=peer_at(e), device_id_type=MESH
                ).start()

    arrived(qbuf, rq)
    pass_on(0)

    def chunk(g, _):
        take(g)

        @pl.when(g + AHEAD < CHUNKS)
        def _():
            send_chunk(g + AHEAD)

        last = g == CHUNKS - 1
        score(0, s_a)
        for i in range(N_QB // 2):
            if i == N_QB // 2 - 1:
                pl.when(jnp.logical_not(last))(lambda: pass_on(g + 1))
            score(2 * i + 1, s_b)
            update(2 * i, s_a)
            pl.when(last)(lambda: give_back(2 * i))
            if i < N_QB // 2 - 1:
                score(2 * i + 2, s_a)
            update(2 * i + 1, s_b)
            pl.when(last)(lambda: give_back(2 * i + 1))
        return 0

    lax.fori_loop(0, CHUNKS, chunk, 0)

    arrived(gbuf.at[pl.ds(1, PEERS - 1)], ro)
    hsrc[...] = jnp.sum(gbuf[...].astype(jnp.float32), axis=0).astype(jnp.bfloat16)
    for dz in range(4):
        pltpu.make_async_remote_copy(
            src_ref=hsrc.at[dz],
            dst_ref=vbuf.at[dz],
            send_sem=ssh,
            recv_sem=rh,
            device_id=source(ys[0] + xs[0] + zs[-dz % 4]),
            device_id_type=MESH,
        ).start()
    arrived(vbuf, rh)
    latents = noisy_s[...] + jnp.sum(vbuf[...].astype(jnp.float32), axis=0)
    patches = latents.astype(jnp.bfloat16)
    xsrc[...] = patches
    xrecv[SEC + sec] = patches
    for d in (-1, 0, 1):
        for s in range(1, SEC) if d == 0 else range(SEC):
            pltpu.make_async_remote_copy(
                src_ref=xsrc,
                dst_ref=xrecv.at[(1 - d) * SEC + sec],
                send_sem=ssx,
                recv_sem=rx,
                device_id=(lax.rem(sec + s, SEC), beside(d)),
                device_id_type=MESH,
            ).start()
    lat_ref[...] = jnp.concatenate([latents[:, :64], latents[:, 64:]], axis=0).T
    arrived(xrecv.at[pl.ds(0, 3 * SEC - 1)], rx)

    for d in range(3):
        got = xrecv[pl.ds(d * SEC, SEC)].reshape(SEC * HALF, 128)
        shifted = [jnp.dot(rowsel_ref[k], got, preferred_element_type=jnp.float32).astype(jnp.bfloat16) for k in range(3)]
        rows = jnp.dot(jnp.concatenate(shifted, axis=1), lanesel_ref[...], preferred_element_type=jnp.float32)
        if d == 0:
            rows = jnp.where(p == 0, 0.0, rows)
        if d == 2:
            rows = jnp.where(p == SEQ - 1, 0.0, rows)
        rows = rows.astype(jnp.bfloat16)
        for f in range(8):
            xf[4 + f, d] = rows[f % 4 * RC : (f % 4 + 1) * RC, f // 4 * 128 : (f // 4 + 1) * 128]
    for l in range(2):
        for f in range(4):
            for a in range(3):
                for n in range(2):
                    lhs[pl.ds((l * 4 + f) * RC, RC), pl.ds(a * 256 + n * 128, 128)] = xf[2 * sec + f + a, l + n]
    row = lax.broadcasted_iota(jnp.int32, (RC, CH), 0)
    is_first = functools.reduce(jnp.logical_or, [row == r * PCOLS for r in range(SEC)])
    is_last = functools.reduce(jnp.logical_or, [row == r * PCOLS + PCOLS - 1 for r in range(SEC)])
    bias, gain = bias_ref[...].reshape(1, CH), vg_ref[...].reshape(1, CH)

    def convolve(n):
        cols = pl.ds(n * CH, CH)
        hid[:, cols] = jnp.dot(lhs[...], wbig[:, cols], preferred_element_type=jnp.float32) + bias

    def activate(n):
        i, j = n // 2, n % 2
        for l in range(2):
            for f in range(4):
                y = 2 * l + i
                x = hid[pl.ds((l * 4 + f) * RC, RC), pl.ds(n * CH, CH)].astype(jnp.bfloat16).astype(jnp.float32)
                x = x * lax.rsqrt(jnp.mean(x * x, axis=-1, keepdims=True) + EPS) * gain
                x = 0.5 * x
                x = x + x * jnp.tanh(x)
                outside = [sec == 0] * (f < 2) + [p == 0] * (y == 0) + [p == SEQ - 1] * (y == 3)
                if outside:
                    x = jnp.where(functools.reduce(jnp.logical_or, outside), 0.0, x)
                tap[f, y, :, pl.ds((1 + j) * CH, CH)] = x.astype(jnp.bfloat16)
                if j == 0:
                    x = jnp.where(is_last, 0.0, pltpu.roll(x, RC - 1, 0))
                    tap[f, y, :, pl.ds(3 * CH, CH)] = x.astype(jnp.bfloat16)
                else:
                    x = jnp.where(is_first, 0.0, pltpu.roll(x, 1, 0))
                    tap[f, y, :, pl.ds(0, CH)] = x.astype(jnp.bfloat16)

    convolve(0)
    for n in range(4):
        if n < 3:
            convolve(n + 1)
        activate(n)

    local[3].wait()
    def one_tap(t):
        a, b = t // 3, t % 3
        block = tap[pl.ds(a, 2), pl.ds(b, 2)].reshape(4 * RC, 4 * CH)
        both = jnp.concatenate([block[:, : 3 * CH], block[:, CH:]], axis=0)
        return jnp.dot(both, wconv[t], preferred_element_type=jnp.float32)

    cacc[...] = one_tap(0) + one_tap(1) + one_tap(2)
    cacc[...] += one_tap(3) + one_tap(4) + one_tap(5)
    cacc[...] += one_tap(6) + one_tap(7) + one_tap(8)
    for f in range(2):
        for y in range(2):
            rows = pl.ds((y * 4 + 2 + f) * RC, RC)
            for j in range(2):
                hidden = hid[rows, pl.ds(((1 - y) * 2 + j) * CH, CH)].astype(jnp.bfloat16).astype(jnp.float32)
                out = hidden + cacc[pl.ds(((j * 2 + f) * 2 + y) * RC, RC), :]
                for r in range(SEC):
                    for n in range(CH // 128):
                        part_out = out[r * PCOLS : (r + 1) * PCOLS, n * 128 : (n + 1) * 128]
                        dec_s[r, f, y, n, pl.ds(j, PCOLS, 2), :] = part_out
            for r in range(SEC):
                for n in range(CH // 128):
                    dec_ref[r, f, y, :, pl.ds(n * 128, 128)] = dec_s[r, f, y, n].astype(jnp.bfloat16)

    arrived(kvsrc, sskv)
    arrived(gsrc.at[pl.ds(1, PEERS - 1)], sso)
    arrived(hsrc, ssh)
    arrived(xrecv.at[pl.ds(0, 3 * SEC - 1)], ssx)

    def sent(g, _):
        arrived(chunk_of(kvbuf, g), ssf.at[g])
        return 0

    lax.fori_loop(0, CHUNKS, sent, 0)


def shards(
    queries, keys, values, query_gain, key_gain, noisy, head_weight, conv_in_weight, conv_in_bias, vae_gain, conv_weight
):
    rowsel, lanesel = gather_constants()
    vmem = pl.BlockSpec(memory_space=pltpu.VMEM)
    anywhere = pl.BlockSpec(memory_space=pl.ANY)
    bf16, f32, dma = jnp.bfloat16, jnp.float32, pltpu.SemaphoreType.DMA
    latents, decoded = pl.pallas_call(
        kernel,
        out_shape=(jax.ShapeDtypeStruct((64, ROWS), f32), jax.ShapeDtypeStruct((SEC, 2, 2, 2 * PCOLS, CH), bf16)),
        in_specs=[anywhere] * 3 + [vmem] * 7 + [anywhere] + [vmem] * 2,
        out_specs=(vmem, vmem),
        scratch_shapes=[
            *[pltpu.VMEM((ROWS, HEADS * HEAD_DIM), bf16)] * 3,
            pltpu.VMEM((HEADS, ROWS, HEAD_DIM), bf16),
            pltpu.VMEM((HEADS, KV_ROWS, HEAD_DIM), bf16),
            pltpu.VMEM((STEPS, ROWS, HEAD_DIM), bf16),
            pltpu.VMEM((STEPS, KV_ROWS, HEAD_DIM), bf16),
            pltpu.VMEM((STEPS, KV_ROWS, HEAD_DIM), bf16),
            pltpu.VMEM((KC, HEAD_DIM), bf16),
            pltpu.VMEM((64, KC), bf16),
            pltpu.VMEM((N_QB, 64, QB), f32),
            pltpu.VMEM((N_QB, 8, QB), f32),
            pltpu.VMEM((N_QB, 8, QB), f32),
            pltpu.VMEM((KC, QB), f32),
            pltpu.VMEM((KC, QB), f32),
            *[pltpu.VMEM((PEERS, 4, HALF, 128), bf16)] * 2,
            *[pltpu.VMEM((4, HALF, 128), bf16)] * 2,
            pltpu.VMEM((HALF, 128), f32),
            pltpu.VMEM((HALF, 128), bf16),
            pltpu.VMEM((3 * SEC, HALF, 128), bf16),
            pltpu.VMEM((12, 3, RC, 128), bf16),
            pltpu.VMEM((8 * RC, 768), bf16),
            pltpu.VMEM((8 * RC, 4 * CH), f32),
            pltpu.VMEM((4, 4, RC, 4 * CH), bf16),
            pltpu.VMEM((768, 4 * CH), bf16),
            pltpu.VMEM((9, 3 * CH, CH), bf16),
            pltpu.VMEM((8 * RC, CH), f32),
            pltpu.VMEM((SEC, 2, 2, CH // 128, 2 * PCOLS, 128), f32),
            dma, dma, dma((CHUNKS,)), dma, dma, dma, dma, dma((CHUNKS,)), dma((CHUNKS,)), dma, dma, dma, dma((4,)),
        ],
        compiler_params=pltpu.CompilerParams(collective_id=0, has_side_effects=True, vmem_limit_bytes=56 * 2**20),
        name="step",
    )(
        queries[0],
        keys[0],
        values[0],
        query_gain.reshape(1, -1),
        key_gain.reshape(1, -1),
        noisy[0].T,
        head_weight.T,
        conv_in_weight.reshape(432, CH),
        conv_in_bias,
        vae_gain,
        conv_weight.reshape(9, 3 * CH, CH),
        jnp.asarray(rowsel, bf16),
        jnp.asarray(lanesel, bf16),
    )
    return latents.T[None], decoded


def solution(mesh):
    placed = (
        P("sec", "seq", None),
        P("sec", "seq", None),
        P("sec", "seq", None),
        P(),
        P(),
        P("sec", "seq", None),
        P(),
        P(),
        P(),
        P(),
        P(),
    )
    return jax.shard_map(
        shards,
        mesh=mesh,
        in_specs=placed,
        out_specs=(P("sec", "seq", None), P(None, "sec", "seq", None, None)),
        check_vma=False,
    )
```

```python
import functools
import math

import jax
import jax.numpy as jnp
import numpy as np
from jax import lax
from jax.experimental import pallas as pl
from jax.experimental.pallas import tpu as pltpu
from jax.sharding import PartitionSpec as P

HEADS = 32
HEAD_DIM = 128
ROWS = 96
HALF = ROWS // 2
SEQ = 64
SEC = 4
STEPS = 32
PER_CHUNK = 4
CHUNKS = STEPS // PER_CHUNK
AHEAD = 3
PER_QB = 8
QB = PER_QB * ROWS
N_QB = STEPS // PER_QB
PEERS = STEPS // 4
KC = 2 * PER_CHUNK * ROWS
KV_ROWS = ROWS + HALF
PCOLS = 12
RC = SEC * PCOLS
CH = 384
EPS = 1e-06
MESH = pl.DeviceIdType.MESH
NT = (((1,), (1,)), ((), ()))
LOG2E = 1.0 / math.log(2.0)


def offsets(i):
    b, c = i // 4, i % 4
    return (b // 4 + c // 2) % 2, (b + c) % 4, c


def gather_constants():
    rows = np.zeros((3, 4 * RC, 4 * RC), np.float32)
    lanes = np.zeros((3, 128, 256), np.float32)
    for k in range(3):
        for f in range(4):
            for r in range(SEC):
                for c in range(PCOLS):
                    if 0 <= c + k - 1 < PCOLS:
                        rows[k, (f * SEC + r) * PCOLS + c, (r * 4 + f) * PCOLS + c + k - 1] = 1
    for half in range(2):
        for i in range(2):
            for tap, (k, j) in enumerate(((0, 1), (1, 0), (1, 1), (2, 0))):
                for ch in range(16):
                    lanes[k, half * 64 + i * 32 + j * 16 + ch, half * 128 + i * 64 + tap * 16 + ch] = 1
    return rows, lanes.reshape(384, 256)


def kernel(
    q_hbm, k_hbm, v_hbm, qg_ref, kg_ref, noisy_ref, hw_hbm, win_hbm, bias_ref, vg_ref, w_hbm, rowsel_hbm, lanesel_hbm,
    lat_ref, dec_ref,
    q_ref, k_ref, v_ref, hw_ref, win_ref, wconv, rowsel_ref, lanesel_ref, qsrc, kvsrc, qbuf, kvbuf, sibbuf, keys, values, acc, m_s, l_s, s_a, s_b, gsrc, gbuf, hsrc, vbuf,
    noisy_s, xsrc, xrecv, xf, lhs, hid, tap, wbig, cacc, dec_s,
    ssq, sskv, ssf, sso, ssh, ssx, rq, rkv, rf, ro, rh, rx, lsem,
):
    sec, p = lax.axis_index("sec"), lax.axis_index("seq")
    z_lo, core = lax.div(sec, 2), lax.rem(sec, 2)
    part, place = lax.div(p, 32), lax.rem(p, 32)
    loads = (
        (q_hbm, q_ref), (k_hbm, k_ref), (v_hbm, v_ref), (hw_hbm, hw_ref),
        (win_hbm, win_ref), (rowsel_hbm, rowsel_ref), (lanesel_hbm, lanesel_ref), (w_hbm, wconv),
    )
    local = [
        pltpu.make_async_copy(src, dst, lsem.at[n])
        for n, (src, dst) in enumerate(loads)
    ]
    for copy in local[:4]:
        copy.start()

    place_y, place_x, place_z = lax.div(place, 16), lax.rem(lax.div(place, 4), 4), lax.rem(place, 4)
    ys = [lax.rem(place_y + n, 2) * 16 for n in range(2)]
    xs = [lax.rem(place_x + n, 4) * 4 for n in range(4)]
    zs = [lax.rem(place_z + n, 4) for n in range(4)]

    def target(h):
        return (2 * z_lo + 1 - part, h + 32 * core)

    def source(j):
        return (2 * z_lo + part, j + 32 * (1 - core))

    def head_at(i):
        dy, dx, dz = offsets(i)
        return ys[dy] + xs[dx] + zs[dz]

    def source_at(i):
        dy, dx, dz = offsets(i)
        return source(ys[dy] + xs[-dx % 4] + zs[-dz % 4])

    def peer_at(e):
        return (sec, ys[e // 4] + xs[-e % 4] + place_z + 32 * part)

    sibling = (2 * z_lo + 1 - core, p)

    def beside(d):
        return lax.rem(p + SEQ + d, SEQ)

    barrier = pltpu.get_barrier_semaphore()
    for i in range(STEPS):
        pl.semaphore_signal(barrier, inc=1, device_id=source_at(i), device_id_type=MESH)
    for d in (-1, 0, 1):
        for s in range(1, SEC) if d == 0 else range(SEC):
            pl.semaphore_signal(barrier, inc=1, device_id=(lax.rem(sec + s, SEC), beside(d)), device_id_type=MESH)

    def normed(ref, gain_ref, factor, store):
        def some(t, _):
            rows = pl.ds(pl.multiple_of(t * 16, 16), 16)
            x = ref[rows, :].astype(jnp.float32)
            scale = lax.rsqrt(jnp.mean(x * x, axis=-1, keepdims=True) + EPS)
            for h in range(HEADS):
                cols = slice(h * HEAD_DIM, (h + 1) * HEAD_DIM)
                y = x[:, cols] * scale * gain_ref[:, cols]
                store(h, rows, (y if factor is None else y * factor).astype(jnp.bfloat16))
            return 0

        lax.fori_loop(0, ROWS // 16, some, 0)

    def store_q(h, rows, y):
        qsrc[h, rows, :] = y

    def store_k(h, rows, y):
        kvsrc[h, rows, :] = y

    local[0].wait()
    normed(q_ref, qg_ref, LOG2E / math.sqrt(HEAD_DIM), store_q)
    pl.semaphore_wait(barrier, STEPS + 3 * SEC - 1)
    for i in range(STEPS):
        h = ys[i // 16] + xs[i // 4 % 4] + zs[i % 4]
        pltpu.make_async_remote_copy(
            src_ref=qsrc.at[h], dst_ref=qbuf.at[i], send_sem=ssq, recv_sem=rq, device_id=target(h), device_id_type=MESH
        ).start()
    for copy in local[4:]:
        copy.start()
    local[1].wait()
    normed(k_ref, kg_ref, None, store_k)
    local[2].wait()
    local[3].wait()
    for h in range(HEADS):
        cols = slice(h * HEAD_DIM, (h + 1) * HEAD_DIM)
        weighted = lax.dot_general(v_ref[:, cols], hw_ref[:, cols], NT, preferred_element_type=jnp.float32)
        kvsrc[h, pl.ds(ROWS, HALF)] = jnp.concatenate([weighted[:HALF], weighted[HALF:]], axis=1).astype(jnp.bfloat16)

    def send_chunk(g):
        for n in range(PER_CHUNK):
            y = lax.rem(place_y + lax.div(g, 4) + n // 2, 2)
            x = lax.rem(place_x + g + n, 4)
            h = y * 16 + x * 4 + zs[n]
            pltpu.make_async_remote_copy(
                src_ref=kvsrc.at[h],
                dst_ref=kvbuf.at[g * PER_CHUNK + n],
                send_sem=sskv,
                recv_sem=rkv.at[g],
                device_id=target(h),
                device_id_type=MESH,
            ).start()

    def arrived(buffer, sem):
        pltpu.make_async_copy(buffer, buffer, sem).wait()

    send_chunk(0)
    wbig[...] = jnp.zeros_like(wbig)
    local[4].wait()
    for a in range(3):
        for b in range(3):
            block = win_ref[pl.ds((a * 3 + b) * 48, 48), :]
            for i in range(2):
                for j in range(2):
                    wbig[pl.ds(a * 256 + (b + i) * 64 + j * 16, 48), pl.ds((i * 2 + j) * CH, CH)] = block
    xf[pl.ds(0, 4)] = jnp.zeros((4,) + xf.shape[1:], jnp.bfloat16)
    noisy = noisy_ref[...].T
    noisy_s[...] = jnp.concatenate([noisy[:HALF], noisy[HALF:]], axis=1)
    acc[...] = jnp.zeros_like(acc)
    l_s[...] = jnp.zeros_like(l_s)
    m_s[...] = jnp.full_like(m_s, -1e30)
    arrived(qsrc, ssq)
    for g in range(1, AHEAD):
        send_chunk(g)

    def chunk_of(buffer, g):
        return buffer.at[pl.ds(g * PER_CHUNK, PER_CHUNK)]

    def pass_on(g):
        arrived(chunk_of(kvbuf, g), rkv.at[g])
        pltpu.make_async_remote_copy(
            src_ref=chunk_of(kvbuf, g),
            dst_ref=chunk_of(sibbuf, g),
            send_sem=ssf.at[g],
            recv_sem=rf.at[g],
            device_id=sibling,
            device_id_type=MESH,
        ).start()

    def take(g):
        arrived(chunk_of(sibbuf, g), rf.at[g])
        steps = pl.ds(g * PER_CHUNK, PER_CHUNK)
        for half in range(2):
            for n, buffer in enumerate((kvbuf, sibbuf)):
                keys[pl.ds((half * 2 + n) * KC // 4, KC // 4), :] = buffer[steps, pl.ds(half * HALF, HALF)].reshape(KC // 4, HEAD_DIM)
        both = jnp.concatenate([buffer[steps, pl.ds(ROWS, HALF)].reshape(KC // 4, 128) for buffer in (kvbuf, sibbuf)], axis=0).T
        values[:, pl.ds(0, KC // 2)] = both[:64]
        values[:, pl.ds(KC // 2, KC // 2)] = both[64:]

    def score(j, dst):
        q = qbuf[pl.ds(j * PER_QB, PER_QB)].reshape(QB, HEAD_DIM)
        dst[...] = lax.dot_general(keys[...], q, NT, preferred_element_type=jnp.float32)

    def update(j, src):
        s = src[...]
        m_old = m_s[j]
        m_new = jnp.maximum(m_old, jnp.max(s, axis=0, keepdims=True))
        m_s[j] = m_new
        alpha = jnp.exp2(m_old - m_new)
        e = jnp.exp2(s - m_new[:1])
        l_s[j] = l_s[j] * alpha + jnp.sum(e.reshape(KC // 8, 8, QB), axis=0)
        acc[j] = acc[j] * alpha[:1] + jnp.dot(values[...], e.astype(jnp.bfloat16), preferred_element_type=jnp.float32)

    def give_back(j):
        total = jnp.sum(l_s[j], axis=0, keepdims=True)
        velocity = (acc[j] * (1.0 / total)).T
        for e in range(j * PER_QB // 4, (j + 1) * PER_QB // 4):
            to = gbuf if e == 0 else gsrc
            for dz in range(4):
                n = e * 4 + dz - j * PER_QB
                rows = velocity[n * ROWS : (n + 1) * ROWS]
                to[e, dz] = jnp.concatenate([rows[:HALF], rows[HALF:]], axis=1).astype(jnp.bfloat16)
            if e:
                pltpu.make_async_remote_copy(
                    src_ref=gsrc.at[e], dst_ref=gbuf.at[e], send_sem=sso, recv_sem=ro, device_id=peer_at(e), device_id_type=MESH
                ).start()

    arrived(qbuf, rq)
    pass_on(0)

    def chunk(g, _):
        take(g)

        @pl.when(g + AHEAD < CHUNKS)
        def _():
            send_chunk(g + AHEAD)

        last = g == CHUNKS - 1
        score(0, s_a)
        for i in range(N_QB // 2):
            if i == N_QB // 2 - 1:
                pl.when(jnp.logical_not(last))(lambda: pass_on(g + 1))
            score(2 * i + 1, s_b)
            update(2 * i, s_a)
            pl.when(last)(lambda: give_back(2 * i))
            if i < N_QB // 2 - 1:
                score(2 * i + 2, s_a)
            update(2 * i + 1, s_b)
            pl.when(last)(lambda: give_back(2 * i + 1))
        return 0

    lax.fori_loop(0, CHUNKS, chunk, 0)

    arrived(gbuf.at[pl.ds(1, PEERS - 1)], ro)
    hsrc[...] = jnp.sum(gbuf[...].astype(jnp.float32), axis=0).astype(jnp.bfloat16)
    for dz in range(4):
        pltpu.make_async_remote_copy(
            src_ref=hsrc.at[dz],
            dst_ref=vbuf.at[dz],
            send_sem=ssh,
            recv_sem=rh,
            device_id=source(ys[0] + xs[0] + zs[-dz % 4]),
            device_id_type=MESH,
        ).start()
    arrived(vbuf, rh)
    latents = noisy_s[...] + jnp.sum(vbuf[...].astype(jnp.float32), axis=0)
    patches = latents.astype(jnp.bfloat16)
    xsrc[...] = patches
    xrecv[SEC + sec] = patches
    for d in (-1, 0, 1):
        for s in range(1, SEC) if d == 0 else range(SEC):
            pltpu.make_async_remote_copy(
                src_ref=xsrc,
                dst_ref=xrecv.at[(1 - d) * SEC + sec],
                send_sem=ssx,
                recv_sem=rx,
                device_id=(lax.rem(sec + s, SEC), beside(d)),
                device_id_type=MESH,
            ).start()
    lat_ref[...] = jnp.concatenate([latents[:, :64], latents[:, 64:]], axis=0).T
    arrived(xrecv.at[pl.ds(0, 3 * SEC - 1)], rx)

    local[5].wait()
    local[6].wait()
    for d in range(3):
        got = xrecv[pl.ds(d * SEC, SEC)].reshape(SEC * HALF, 128)
        shifted = [jnp.dot(rowsel_ref[k], got, preferred_element_type=jnp.float32).astype(jnp.bfloat16) for k in range(3)]
        rows = jnp.dot(jnp.concatenate(shifted, axis=1), lanesel_ref[...], preferred_element_type=jnp.float32)
        if d == 0:
            rows = jnp.where(p == 0, 0.0, rows)
        if d == 2:
            rows = jnp.where(p == SEQ - 1, 0.0, rows)
        rows = rows.astype(jnp.bfloat16)
        for f in range(8):
            xf[4 + f, d] = rows[f % 4 * RC : (f % 4 + 1) * RC, f // 4 * 128 : (f // 4 + 1) * 128]
    for l in range(2):
        for f in range(4):
            for a in range(3):
                for n in range(2):
                    lhs[pl.ds((l * 4 + f) * RC, RC), pl.ds(a * 256 + n * 128, 128)] = xf[2 * sec + f + a, l + n]
    row = lax.broadcasted_iota(jnp.int32, (RC, CH), 0)
    is_first = functools.reduce(jnp.logical_or, [row == r * PCOLS for r in range(SEC)])
    is_last = functools.reduce(jnp.logical_or, [row == r * PCOLS + PCOLS - 1 for r in range(SEC)])
    bias, gain = bias_ref[...].reshape(1, CH), vg_ref[...].reshape(1, CH)

    def convolve(n):
        cols = pl.ds(n * CH, CH)
        hid[:, cols] = jnp.dot(lhs[...], wbig[:, cols], preferred_element_type=jnp.float32) + bias

    def activate(n):
        i, j = n // 2, n % 2
        for l in range(2):
            for f in range(4):
                y = 2 * l + i
                x = hid[pl.ds((l * 4 + f) * RC, RC), pl.ds(n * CH, CH)].astype(jnp.bfloat16).astype(jnp.float32)
                x = x * lax.rsqrt(jnp.mean(x * x, axis=-1, keepdims=True) + EPS) * gain
                x = 0.5 * x
                x = x + x * jnp.tanh(x)
                outside = [sec == 0] * (f < 2) + [p == 0] * (y == 0) + [p == SEQ - 1] * (y == 3)
                if outside:
                    x = jnp.where(functools.reduce(jnp.logical_or, outside), 0.0, x)
                tap[f, y, :, pl.ds((1 + j) * CH, CH)] = x.astype(jnp.bfloat16)
                if j == 0:
                    x = jnp.where(is_last, 0.0, pltpu.roll(x, RC - 1, 0))
                    tap[f, y, :, pl.ds(3 * CH, CH)] = x.astype(jnp.bfloat16)
                else:
                    x = jnp.where(is_first, 0.0, pltpu.roll(x, 1, 0))
                    tap[f, y, :, pl.ds(0, CH)] = x.astype(jnp.bfloat16)

    convolve(0)
    for n in range(4):
        if n < 3:
            convolve(n + 1)
        activate(n)

    local[7].wait()
    def one_tap(t):
        a, b = t // 3, t % 3
        block = tap[pl.ds(a, 2), pl.ds(b, 2)].reshape(4 * RC, 4 * CH)
        both = jnp.concatenate([block[:, : 3 * CH], block[:, CH:]], axis=0)
        return jnp.dot(both, wconv[t], preferred_element_type=jnp.float32)

    cacc[...] = one_tap(0) + one_tap(1) + one_tap(2)
    cacc[...] += one_tap(3) + one_tap(4) + one_tap(5)
    cacc[...] += one_tap(6) + one_tap(7) + one_tap(8)
    for f in range(2):
        for y in range(2):
            rows = pl.ds((y * 4 + 2 + f) * RC, RC)
            for j in range(2):
                hidden = hid[rows, pl.ds(((1 - y) * 2 + j) * CH, CH)].astype(jnp.bfloat16).astype(jnp.float32)
                out = hidden + cacc[pl.ds(((j * 2 + f) * 2 + y) * RC, RC), :]
                for r in range(SEC):
                    for n in range(CH // 128):
                        part_out = out[r * PCOLS : (r + 1) * PCOLS, n * 128 : (n + 1) * 128]
                        dec_s[r, f, y, n, pl.ds(j, PCOLS, 2), :] = part_out
            for r in range(SEC):
                for n in range(CH // 128):
                    dec_ref[r, f, y, :, pl.ds(n * 128, 128)] = dec_s[r, f, y, n].astype(jnp.bfloat16)

    arrived(kvsrc, sskv)
    arrived(gsrc.at[pl.ds(1, PEERS - 1)], sso)
    arrived(hsrc, ssh)
    arrived(xrecv.at[pl.ds(0, 3 * SEC - 1)], ssx)

    def sent(g, _):
        arrived(chunk_of(kvbuf, g), ssf.at[g])
        return 0

    lax.fori_loop(0, CHUNKS, sent, 0)


def hand_on(lat_ref, dec_ref, lat_out, dec_out, sems):
    copies = [pltpu.make_async_copy(lat_ref, lat_out, sems.at[0]), pltpu.make_async_copy(dec_ref, dec_out, sems.at[1])]
    for copy in copies:
        copy.start()
    for copy in copies:
        copy.wait()


def shards(
    queries, keys, values, query_gain, key_gain, noisy, head_weight, conv_in_weight, conv_in_bias, vae_gain, conv_weight
):
    rowsel, lanesel = gather_constants()
    vmem = pl.BlockSpec(memory_space=pltpu.VMEM)
    anywhere = pl.BlockSpec(memory_space=pl.ANY)
    bf16, f32, dma = jnp.bfloat16, jnp.float32, pltpu.SemaphoreType.DMA
    latents, decoded = pl.pallas_call(
        kernel,
        out_shape=(jax.ShapeDtypeStruct((64, ROWS), f32), jax.ShapeDtypeStruct((SEC, 2, 2, 2 * PCOLS, CH), bf16)),
        in_specs=[anywhere] * 3 + [vmem] * 3 + [anywhere] * 2 + [vmem] * 2 + [anywhere] * 3,
        out_specs=(vmem, vmem),
        scratch_shapes=[
            *[pltpu.VMEM((ROWS, HEADS * HEAD_DIM), bf16)] * 3,
            pltpu.VMEM((64, HEADS * HEAD_DIM), bf16),
            pltpu.VMEM((432, CH), bf16),
            pltpu.VMEM((9, 3 * CH, CH), bf16),
            pltpu.VMEM((3, 4 * RC, 4 * RC), bf16),
            pltpu.VMEM((384, 256), bf16),
            pltpu.VMEM((HEADS, ROWS, HEAD_DIM), bf16),
            pltpu.VMEM((HEADS, KV_ROWS, HEAD_DIM), bf16),
            pltpu.VMEM((STEPS, ROWS, HEAD_DIM), bf16),
            pltpu.VMEM((STEPS, KV_ROWS, HEAD_DIM), bf16),
            pltpu.VMEM((STEPS, KV_ROWS, HEAD_DIM), bf16),
            pltpu.VMEM((KC, HEAD_DIM), bf16),
            pltpu.VMEM((64, KC), bf16),
            pltpu.VMEM((N_QB, 64, QB), f32),
            pltpu.VMEM((N_QB, 8, QB), f32),
            pltpu.VMEM((N_QB, 8, QB), f32),
            pltpu.VMEM((KC, QB), f32),
            pltpu.VMEM((KC, QB), f32),
            *[pltpu.VMEM((PEERS, 4, HALF, 128), bf16)] * 2,
            *[pltpu.VMEM((4, HALF, 128), bf16)] * 2,
            pltpu.VMEM((HALF, 128), f32),
            pltpu.VMEM((HALF, 128), bf16),
            pltpu.VMEM((3 * SEC, HALF, 128), bf16),
            pltpu.VMEM((12, 3, RC, 128), bf16),
            pltpu.VMEM((8 * RC, 768), bf16),
            pltpu.VMEM((8 * RC, 4 * CH), f32),
            pltpu.VMEM((4, 4, RC, 4 * CH), bf16),
            pltpu.VMEM((768, 4 * CH), bf16),
            pltpu.VMEM((8 * RC, CH), f32),
            pltpu.VMEM((SEC, 2, 2, CH // 128, 2 * PCOLS, 128), f32),
            dma, dma, dma((CHUNKS,)), dma, dma, dma, dma, dma((CHUNKS,)), dma((CHUNKS,)), dma, dma, dma, dma((8,)),
        ],
        compiler_params=pltpu.CompilerParams(collective_id=0, has_side_effects=True, vmem_limit_bytes=56 * 2**20),
        name="step",
    )(
        queries[0],
        keys[0],
        values[0],
        query_gain.reshape(1, -1),
        key_gain.reshape(1, -1),
        noisy[0].T,
        head_weight.T,
        conv_in_weight.reshape(432, CH),
        conv_in_bias,
        vae_gain,
        conv_weight.reshape(9, 3 * CH, CH),
        jnp.asarray(rowsel, bf16),
        jnp.asarray(lanesel, bf16),
    )
    latents, decoded = pl.pallas_call(
        hand_on,
        out_shape=(jax.ShapeDtypeStruct(latents.shape, f32), jax.ShapeDtypeStruct(decoded.shape, bf16)),
        in_specs=[pl.BlockSpec(memory_space=pltpu.HBM)] * 2,
        out_specs=(anywhere, anywhere),
        scratch_shapes=[dma((2,))],
        name="hand_on",
    )(latents, decoded)
    return latents.T[None], decoded


def solution(mesh):
    placed = (
        P("sec", "seq", None),
        P("sec", "seq", None),
        P("sec", "seq", None),
        P(),
        P(),
        P("sec", "seq", None),
        P(),
        P(),
        P(),
        P(),
        P(),
    )
    return jax.shard_map(
        shards,
        mesh=mesh,
        in_specs=placed,
        out_specs=(P("sec", "seq", None), P(None, "sec", "seq", None, None)),
        check_vma=False,
    )
```

```python
import functools
import math

import jax
import jax.numpy as jnp
import numpy as np
from jax import lax
from jax.experimental import pallas as pl
from jax.experimental.pallas import tpu as pltpu
from jax.sharding import PartitionSpec as P

HEADS = 32
HEAD_DIM = 128
ROWS = 96
HALF = ROWS // 2
SEQ = 64
SEC = 4
STEPS = 32
PER_CHUNK = 4
CHUNKS = STEPS // PER_CHUNK
EARLY = CHUNKS // 2
PER_QB = 8
QB = PER_QB * ROWS
N_QB = STEPS // PER_QB
PEERS = STEPS // 4
KC = 2 * PER_CHUNK * ROWS
KV_ROWS = ROWS + HALF
PCOLS = 12
RC = SEC * PCOLS
CH = 384
EPS = 1e-06
MESH = pl.DeviceIdType.MESH
NT = (((1,), (1,)), ((), ()))
LOG2E = 1.0 / math.log(2.0)


def offsets(i):
    b, c = i // 4, i % 4
    return (b // 4 + c // 2) % 2, (b + c) % 4, c


def gather_constants():
    rows = np.zeros((3, 4 * RC, 4 * RC), np.float32)
    lanes = np.zeros((3, 128, 256), np.float32)
    for k in range(3):
        for f in range(4):
            for r in range(SEC):
                for c in range(PCOLS):
                    if 0 <= c + k - 1 < PCOLS:
                        rows[k, (f * SEC + r) * PCOLS + c, (r * 4 + f) * PCOLS + c + k - 1] = 1
    for half in range(2):
        for i in range(2):
            for tap, (k, j) in enumerate(((0, 1), (1, 0), (1, 1), (2, 0))):
                for ch in range(16):
                    lanes[k, half * 64 + i * 32 + j * 16 + ch, half * 128 + i * 64 + tap * 16 + ch] = 1
    return rows, lanes.reshape(384, 256)


def kernel(
    q_hbm, k_hbm, v_hbm, qg_ref, kg_ref, noisy_ref, hw_hbm, win_hbm, bias_ref, vg_ref, w_hbm, rowsel_hbm, lanesel_hbm,
    lat_ref, dec_ref,
    q_ref, k_ref, v_ref, hw_ref, win_ref, wconv, rowsel_ref, lanesel_ref, qsrc, kvsrc, qbuf, kvbuf, sibbuf, keys, values, acc, m_s, l_s, s_a, s_b, gsrc, gbuf, hsrc, vbuf,
    noisy_s, xsrc, xrecv, xf, lhs, hid, tap, wbig, cacc, dec_s,
    ssq, sskv, ssf, sso, ssh, ssx, rq, rkv, rf, ro, rh, rx, lsem,
):
    sec, p = lax.axis_index("sec"), lax.axis_index("seq")
    z_lo, core = lax.div(sec, 2), lax.rem(sec, 2)
    part, place = lax.div(p, 32), lax.rem(p, 32)
    loads = (
        (q_hbm, q_ref), (k_hbm, k_ref), (v_hbm, v_ref), (hw_hbm, hw_ref),
        (win_hbm, win_ref), (rowsel_hbm, rowsel_ref), (lanesel_hbm, lanesel_ref), (w_hbm, wconv),
    )
    local = [
        pltpu.make_async_copy(src, dst, lsem.at[n])
        for n, (src, dst) in enumerate(loads)
    ]
    for copy in local[:4]:
        copy.start()

    place_y, place_x, place_z = lax.div(place, 16), lax.rem(lax.div(place, 4), 4), lax.rem(place, 4)
    ys = [lax.rem(place_y + n, 2) * 16 for n in range(2)]
    xs = [lax.rem(place_x + n, 4) * 4 for n in range(4)]
    zs = [lax.rem(place_z + n, 4) for n in range(4)]

    def target(h):
        return (2 * z_lo + 1 - part, h + 32 * core)

    def source(j):
        return (2 * z_lo + part, j + 32 * (1 - core))

    def head_at(i):
        dy, dx, dz = offsets(i)
        return ys[dy] + xs[dx] + zs[dz]

    def source_at(i):
        dy, dx, dz = offsets(i)
        return source(ys[dy] + xs[-dx % 4] + zs[-dz % 4])

    def peer_at(e):
        y = lax.rem(place_y + lax.div(e, 4), 2)
        x = lax.rem(place_x + 8 - e, 4)
        return (sec, y * 16 + x * 4 + place_z + 32 * part)

    sibling = (2 * z_lo + 1 - core, p)

    def beside(d):
        return lax.rem(p + SEQ + d, SEQ)

    barrier = pltpu.get_barrier_semaphore()
    for i in range(STEPS):
        pl.semaphore_signal(barrier, inc=1, device_id=source_at(i), device_id_type=MESH)
    for d in (-1, 0, 1):
        for s in range(1, SEC) if d == 0 else range(SEC):
            pl.semaphore_signal(barrier, inc=1, device_id=(lax.rem(sec + s, SEC), beside(d)), device_id_type=MESH)

    def normed(ref, gain_ref, factor, store):
        def some(t, _):
            rows = pl.ds(pl.multiple_of(t * 16, 16), 16)
            x = ref[rows, :].astype(jnp.float32)
            scale = lax.rsqrt(jnp.mean(x * x, axis=-1, keepdims=True) + EPS)
            for h in range(HEADS):
                cols = slice(h * HEAD_DIM, (h + 1) * HEAD_DIM)
                y = x[:, cols] * scale * gain_ref[:, cols]
                store(h, rows, (y if factor is None else y * factor).astype(jnp.bfloat16))
            return 0

        lax.fori_loop(0, ROWS // 16, some, 0)

    def store_q(h, rows, y):
        qsrc[h, rows, :] = y

    def store_k(h, rows, y):
        kvsrc[h, rows, :] = y

    local[0].wait()
    normed(q_ref, qg_ref, LOG2E / math.sqrt(HEAD_DIM), store_q)
    pl.semaphore_wait(barrier, STEPS + 3 * SEC - 1)
    def send_queries(j):
        for n in range(PER_QB):
            e, i = 2 * j + n // 4, j * PER_QB + n
            h = lax.rem(place_y + lax.div(e, 4), 2) * 16 + lax.rem(place_x + e, 4) * 4 + zs[n % 4]
            pltpu.make_async_remote_copy(
                src_ref=qsrc.at[h],
                dst_ref=qbuf.at[i],
                send_sem=ssq.at[j],
                recv_sem=rq.at[j],
                device_id=target(h),
                device_id_type=MESH,
            ).start()

    send_queries(0)
    for copy in local[4:]:
        copy.start()
    local[1].wait()
    normed(k_ref, kg_ref, None, store_k)
    local[2].wait()
    local[3].wait()
    for h in range(HEADS):
        cols = slice(h * HEAD_DIM, (h + 1) * HEAD_DIM)
        weighted = lax.dot_general(v_ref[:, cols], hw_ref[:, cols], NT, preferred_element_type=jnp.float32)
        kvsrc[h, pl.ds(ROWS, HALF)] = jnp.concatenate([weighted[:HALF], weighted[HALF:]], axis=1).astype(jnp.bfloat16)

    def send_chunk(g):
        for n in range(PER_CHUNK):
            y = lax.rem(place_y + lax.div(g, 4) + n // 2, 2)
            x = lax.rem(place_x + g + n, 4)
            h = y * 16 + x * 4 + zs[n]
            pltpu.make_async_remote_copy(
                src_ref=kvsrc.at[h],
                dst_ref=kvbuf.at[g * PER_CHUNK + n],
                send_sem=sskv.at[g],
                recv_sem=rkv.at[g],
                device_id=target(h),
                device_id_type=MESH,
            ).start()

    def arrived(buffer, sem):
        pltpu.make_async_copy(buffer, buffer, sem).wait()

    def chunk_of(buffer, g):
        return buffer.at[pl.ds(g * PER_CHUNK, PER_CHUNK)]

    def queries_of(buffer, j):
        return buffer.at[pl.ds(j * PER_QB, PER_QB)]

    def sent_queries(j):
        arrived(queries_of(qsrc, j), ssq.at[j])

    def sent_chunk(g):
        arrived(chunk_of(kvsrc, g), sskv.at[g])

    send_chunk(0)
    send_chunk(1)
    wbig[...] = jnp.zeros_like(wbig)
    local[4].wait()
    for a in range(3):
        for b in range(3):
            block = win_ref[pl.ds((a * 3 + b) * 48, 48), :]
            for i in range(2):
                for j in range(2):
                    wbig[pl.ds(a * 256 + (b + i) * 64 + j * 16, 48), pl.ds((i * 2 + j) * CH, CH)] = block
    xf[pl.ds(0, 4)] = jnp.zeros((4,) + xf.shape[1:], jnp.bfloat16)
    noisy = noisy_ref[...].T
    noisy_s[...] = jnp.concatenate([noisy[:HALF], noisy[HALF:]], axis=1)
    acc[...] = jnp.zeros_like(acc)
    l_s[...] = jnp.zeros_like(l_s)
    m_s[...] = jnp.full_like(m_s, -1e30)
    sent_queries(0)
    send_chunk(2)
    sent_chunk(0)
    send_chunk(3)
    sent_chunk(1)
    send_queries(1)

    def pass_on(g):
        arrived(chunk_of(kvbuf, g), rkv.at[g])
        pltpu.make_async_remote_copy(
            src_ref=chunk_of(kvbuf, g),
            dst_ref=chunk_of(sibbuf, g),
            send_sem=ssf.at[g],
            recv_sem=rf.at[g],
            device_id=sibling,
            device_id_type=MESH,
        ).start()

    def take(g):
        arrived(chunk_of(sibbuf, g), rf.at[g])
        steps = pl.ds(g * PER_CHUNK, PER_CHUNK)
        for half in range(2):
            for n, buffer in enumerate((kvbuf, sibbuf)):
                keys[g, pl.ds((half * 2 + n) * KC // 4, KC // 4), :] = buffer[steps, pl.ds(half * HALF, HALF)].reshape(KC // 4, HEAD_DIM)
        both = jnp.concatenate([buffer[steps, pl.ds(ROWS, HALF)].reshape(KC // 4, 128) for buffer in (kvbuf, sibbuf)], axis=0).T
        values[g, :, pl.ds(0, KC // 2)] = both[:64]
        values[g, :, pl.ds(KC // 2, KC // 2)] = both[64:]

    def score(g, j, dst):
        q = qbuf[pl.ds(j * PER_QB, PER_QB)].reshape(QB, HEAD_DIM)
        dst[...] = lax.dot_general(keys[g], q, NT, preferred_element_type=jnp.float32)

    def update(g, j, src):
        s = src[...]
        m_old = m_s[j]
        m_new = jnp.maximum(m_old, jnp.max(s, axis=0, keepdims=True))
        m_s[j] = m_new
        alpha = jnp.exp2(m_old - m_new)
        e = jnp.exp2(s - m_new[:1])
        l_s[j] = l_s[j] * alpha + jnp.sum(e.reshape(KC // 8, 8, QB), axis=0)
        acc[j] = acc[j] * alpha[:1] + jnp.dot(values[g], e.astype(jnp.bfloat16), preferred_element_type=jnp.float32)

    def give_back(j):
        total = jnp.sum(l_s[j], axis=0, keepdims=True)
        velocity = (acc[j] * (1.0 / total)).T
        for u in range(PER_QB // 4):
            e = j * (PER_QB // 4) + u
            for dz in range(4):
                rows = velocity[(u * 4 + dz) * ROWS : (u * 4 + dz + 1) * ROWS]
                gsrc[e, dz] = jnp.concatenate([rows[:HALF], rows[HALF:]], axis=1).astype(jnp.bfloat16)

            @pl.when(e == 0)
            def _():
                gbuf[0] = gsrc[0]

            @pl.when(e > 0)
            def _():
                pltpu.make_async_remote_copy(
                    src_ref=gsrc.at[e], dst_ref=gbuf.at[e], send_sem=sso, recv_sem=ro, device_id=peer_at(e), device_id_type=MESH
                ).start()

    for g in range(EARLY):
        pass_on(g)
        if g == 2:
            sent_chunk(2)
            send_queries(2)
    for g in range(EARLY):
        take(g)
    arrived(queries_of(qbuf, 0), rq.at[0])

    n_steps = CHUNKS * N_QB
    n_early = EARLY * N_QB

    def place_of(t):
        early = t < n_early
        major, minor = lax.div(t, 4), lax.rem(t, 4)
        return jnp.where(early, minor, major), jnp.where(early, major, minor)

    def step(t, now, then):
        g, j = place_of(t)
        after = jnp.minimum(t + 1, n_steps - 1)
        g_after, j_after = place_of(after)
        starts = lax.rem(t, 4) == 0

        @pl.when(t == 0)
        def _():
            sent_chunk(3)
            send_queries(3)

        @pl.when(jnp.logical_and(starts, jnp.logical_and(t > 0, t < n_early)))
        def _():
            sent_queries(j)
            send_chunk(j + 3)

        @pl.when(t == n_early)
        def _():
            sent_chunk(4)
            send_chunk(7)

        @pl.when(jnp.logical_and(lax.rem(t, 4) == 3, t + 1 < n_early))
        def _():
            arrived(queries_of(qbuf, j_after), rq.at[j_after])

        @pl.when(jnp.logical_and(lax.rem(t, 4) == 3, jnp.logical_and(t + 1 >= n_early, t + 1 < n_steps)))
        def _():
            take(g_after)

        score(g_after, j_after, then)
        update(g, j, now)

        @pl.when(t >= n_steps - N_QB)
        def _():
            give_back(j)

        @pl.when(jnp.logical_or(t == n_early - 2, jnp.logical_and(lax.rem(t, 4) == 1, jnp.logical_and(t > n_early, t < n_steps - 4))))
        def _():
            pass_on(lax.div(t + 3, 4))

    score(0, 0, s_a)

    def two_steps(n, _):
        step(2 * n, s_a, s_b)
        step(2 * n + 1, s_b, s_a)
        return 0

    lax.fori_loop(0, n_steps // 2, two_steps, 0)

    arrived(gbuf.at[pl.ds(1, PEERS - 1)], ro)
    hsrc[...] = jnp.sum(gbuf[...].astype(jnp.float32), axis=0).astype(jnp.bfloat16)
    for dz in range(4):
        pltpu.make_async_remote_copy(
            src_ref=hsrc.at[dz],
            dst_ref=vbuf.at[dz],
            send_sem=ssh,
            recv_sem=rh,
            device_id=source(ys[0] + xs[0] + zs[-dz % 4]),
            device_id_type=MESH,
        ).start()
    arrived(vbuf, rh)
    latents = noisy_s[...] + jnp.sum(vbuf[...].astype(jnp.float32), axis=0)
    patches = latents.astype(jnp.bfloat16)
    xsrc[...] = patches
    xrecv[SEC + sec] = patches
    for d in (-1, 0, 1):
        for s in range(1, SEC) if d == 0 else range(SEC):
            pltpu.make_async_remote_copy(
                src_ref=xsrc,
                dst_ref=xrecv.at[(1 - d) * SEC + sec],
                send_sem=ssx,
                recv_sem=rx,
                device_id=(lax.rem(sec + s, SEC), beside(d)),
                device_id_type=MESH,
            ).start()
    lat_ref[...] = jnp.concatenate([latents[:, :64], latents[:, 64:]], axis=0).T
    arrived(xrecv.at[pl.ds(0, 3 * SEC - 1)], rx)

    local[5].wait()
    local[6].wait()
    for d in range(3):
        got = xrecv[pl.ds(d * SEC, SEC)].reshape(SEC * HALF, 128)
        shifted = [jnp.dot(rowsel_ref[k], got, preferred_element_type=jnp.float32).astype(jnp.bfloat16) for k in range(3)]
        rows = jnp.dot(jnp.concatenate(shifted, axis=1), lanesel_ref[...], preferred_element_type=jnp.float32)
        if d == 0:
            rows = jnp.where(p == 0, 0.0, rows)
        if d == 2:
            rows = jnp.where(p == SEQ - 1, 0.0, rows)
        rows = rows.astype(jnp.bfloat16)
        for f in range(8):
            xf[4 + f, d] = rows[f % 4 * RC : (f % 4 + 1) * RC, f // 4 * 128 : (f // 4 + 1) * 128]
    for l in range(2):
        for f in range(4):
            for a in range(3):
                for n in range(2):
                    lhs[pl.ds((l * 4 + f) * RC, RC), pl.ds(a * 256 + n * 128, 128)] = xf[2 * sec + f + a, l + n]
    row = lax.broadcasted_iota(jnp.int32, (RC, CH), 0)
    is_first = functools.reduce(jnp.logical_or, [row == r * PCOLS for r in range(SEC)])
    is_last = functools.reduce(jnp.logical_or, [row == r * PCOLS + PCOLS - 1 for r in range(SEC)])
    bias, gain = bias_ref[...].reshape(1, CH), vg_ref[...].reshape(1, CH)

    def convolve(n):
        cols = pl.ds(n * CH, CH)
        hid[:, cols] = jnp.dot(lhs[...], wbig[:, cols], preferred_element_type=jnp.float32) + bias

    def activate(n):
        i, j = n // 2, n % 2
        for l in range(2):
            for f in range(4):
                y = 2 * l + i
                x = hid[pl.ds((l * 4 + f) * RC, RC), pl.ds(n * CH, CH)].astype(jnp.bfloat16).astype(jnp.float32)
                x = x * lax.rsqrt(jnp.mean(x * x, axis=-1, keepdims=True) + EPS) * gain
                x = 0.5 * x
                x = x + x * jnp.tanh(x)
                outside = [sec == 0] * (f < 2) + [p == 0] * (y == 0) + [p == SEQ - 1] * (y == 3)
                if outside:
                    x = jnp.where(functools.reduce(jnp.logical_or, outside), 0.0, x)
                tap[f, y, :, pl.ds((1 + j) * CH, CH)] = x.astype(jnp.bfloat16)
                if j == 0:
                    x = jnp.where(is_last, 0.0, pltpu.roll(x, RC - 1, 0))
                    tap[f, y, :, pl.ds(3 * CH, CH)] = x.astype(jnp.bfloat16)
                else:
                    x = jnp.where(is_first, 0.0, pltpu.roll(x, 1, 0))
                    tap[f, y, :, pl.ds(0, CH)] = x.astype(jnp.bfloat16)

    convolve(0)
    for n in range(4):
        if n < 3:
            convolve(n + 1)
        activate(n)

    local[7].wait()
    def one_tap(t):
        a, b = t // 3, t % 3
        block = tap[pl.ds(a, 2), pl.ds(b, 2)].reshape(4 * RC, 4 * CH)
        both = jnp.concatenate([block[:, : 3 * CH], block[:, CH:]], axis=0)
        return jnp.dot(both, wconv[t], preferred_element_type=jnp.float32)

    cacc[...] = one_tap(0) + one_tap(1) + one_tap(2)
    cacc[...] += one_tap(3) + one_tap(4) + one_tap(5)
    cacc[...] += one_tap(6) + one_tap(7) + one_tap(8)
    for f in range(2):
        for y in range(2):
            rows = pl.ds((y * 4 + 2 + f) * RC, RC)
            for j in range(2):
                hidden = hid[rows, pl.ds(((1 - y) * 2 + j) * CH, CH)].astype(jnp.bfloat16).astype(jnp.float32)
                out = hidden + cacc[pl.ds(((j * 2 + f) * 2 + y) * RC, RC), :]
                for r in range(SEC):
                    for n in range(CH // 128):
                        part_out = out[r * PCOLS : (r + 1) * PCOLS, n * 128 : (n + 1) * 128]
                        dec_s[r, f, y, n, pl.ds(j, PCOLS, 2), :] = part_out
            for r in range(SEC):
                for n in range(CH // 128):
                    dec_ref[r, f, y, :, pl.ds(n * 128, 128)] = dec_s[r, f, y, n].astype(jnp.bfloat16)

    for g in range(5, CHUNKS):
        sent_chunk(g)
    arrived(gsrc.at[pl.ds(1, PEERS - 1)], sso)
    arrived(hsrc, ssh)
    arrived(xrecv.at[pl.ds(0, 3 * SEC - 1)], ssx)

    def sent(g, _):
        arrived(chunk_of(kvbuf, g), ssf.at[g])
        return 0

    lax.fori_loop(0, CHUNKS, sent, 0)


def hand_on(lat_ref, dec_ref, lat_out, dec_out):
    lat_out[...] = lat_ref[...]
    dec_out[...] = dec_ref[...]


def shards(
    queries, keys, values, query_gain, key_gain, noisy, head_weight, conv_in_weight, conv_in_bias, vae_gain, conv_weight
):
    rowsel, lanesel = gather_constants()
    vmem = pl.BlockSpec(memory_space=pltpu.VMEM)
    anywhere = pl.BlockSpec(memory_space=pl.ANY)
    bf16, f32, dma = jnp.bfloat16, jnp.float32, pltpu.SemaphoreType.DMA
    latents, decoded = pl.pallas_call(
        kernel,
        out_shape=(jax.ShapeDtypeStruct((64, ROWS), f32), jax.ShapeDtypeStruct((SEC, 2, 2, 2 * PCOLS, CH), bf16)),
        in_specs=[anywhere] * 3 + [vmem] * 3 + [anywhere] * 2 + [vmem] * 2 + [anywhere] * 3,
        out_specs=(vmem, vmem),
        scratch_shapes=[
            *[pltpu.VMEM((ROWS, HEADS * HEAD_DIM), bf16)] * 3,
            pltpu.VMEM((64, HEADS * HEAD_DIM), bf16),
            pltpu.VMEM((432, CH), bf16),
            pltpu.VMEM((9, 3 * CH, CH), bf16),
            pltpu.VMEM((3, 4 * RC, 4 * RC), bf16),
            pltpu.VMEM((384, 256), bf16),
            pltpu.VMEM((HEADS, ROWS, HEAD_DIM), bf16),
            pltpu.VMEM((HEADS, KV_ROWS, HEAD_DIM), bf16),
            pltpu.VMEM((STEPS, ROWS, HEAD_DIM), bf16),
            pltpu.VMEM((STEPS, KV_ROWS, HEAD_DIM), bf16),
            pltpu.VMEM((STEPS, KV_ROWS, HEAD_DIM), bf16),
            pltpu.VMEM((CHUNKS, KC, HEAD_DIM), bf16),
            pltpu.VMEM((CHUNKS, 64, KC), bf16),
            pltpu.VMEM((N_QB, 64, QB), f32),
            pltpu.VMEM((N_QB, 8, QB), f32),
            pltpu.VMEM((N_QB, 8, QB), f32),
            pltpu.VMEM((KC, QB), f32),
            pltpu.VMEM((KC, QB), f32),
            *[pltpu.VMEM((PEERS, 4, HALF, 128), bf16)] * 2,
            *[pltpu.VMEM((4, HALF, 128), bf16)] * 2,
            pltpu.VMEM((HALF, 128), f32),
            pltpu.VMEM((HALF, 128), bf16),
            pltpu.VMEM((3 * SEC, HALF, 128), bf16),
            pltpu.VMEM((12, 3, RC, 128), bf16),
            pltpu.VMEM((8 * RC, 768), bf16),
            pltpu.VMEM((8 * RC, 4 * CH), f32),
            pltpu.VMEM((4, 4, RC, 4 * CH), bf16),
            pltpu.VMEM((768, 4 * CH), bf16),
            pltpu.VMEM((8 * RC, CH), f32),
            pltpu.VMEM((SEC, 2, 2, CH // 128, 2 * PCOLS, 128), f32),
            dma((N_QB,)), dma((CHUNKS,)), dma((CHUNKS,)), dma, dma, dma, dma((N_QB,)), dma((CHUNKS,)), dma((CHUNKS,)), dma, dma, dma, dma((8,)),
        ],
        compiler_params=pltpu.CompilerParams(collective_id=0, has_side_effects=True, vmem_limit_bytes=56 * 2**20),
        name="step",
    )(
        queries[0],
        keys[0],
        values[0],
        query_gain.reshape(1, -1),
        key_gain.reshape(1, -1),
        noisy[0].T,
        head_weight.T,
        conv_in_weight.reshape(432, CH),
        conv_in_bias,
        vae_gain,
        conv_weight.reshape(9, 3 * CH, CH),
        jnp.asarray(rowsel, bf16),
        jnp.asarray(lanesel, bf16),
    )
    latents, decoded = pl.pallas_call(
        hand_on,
        out_shape=(jax.ShapeDtypeStruct(latents.shape, f32), jax.ShapeDtypeStruct(decoded.shape, bf16)),
        in_specs=[vmem] * 2,
        out_specs=(vmem, vmem),
        name="hand_on",
    )(latents, decoded)
    return latents.T[None], decoded


def solution(mesh):
    placed = (
        P("sec", "seq", None),
        P("sec", "seq", None),
        P("sec", "seq", None),
        P(),
        P(),
        P("sec", "seq", None),
        P(),
        P(),
        P(),
        P(),
        P(),
    )
    return jax.shard_map(
        shards,
        mesh=mesh,
        in_specs=placed,
        out_specs=(P("sec", "seq", None), P(None, "sec", "seq", None, None)),
        check_vma=False,
    )
```

```python
import functools
import math

import jax
import jax.numpy as jnp
import numpy as np
from jax import lax
from jax.experimental import pallas as pl
from jax.experimental.pallas import tpu as pltpu
from jax.sharding import PartitionSpec as P

HEADS = 32
HEAD_DIM = 128
ROWS = 96
HALF = ROWS // 2
SEQ = 64
SEC = 4
STEPS = 32
PER_CHUNK = 4
CHUNKS = STEPS // PER_CHUNK
EARLY = CHUNKS // 2
PER_QB = 8
QB = PER_QB * ROWS
N_QB = STEPS // PER_QB
PEERS = STEPS // 4
KC = 2 * PER_CHUNK * ROWS
KV_ROWS = ROWS + HALF
PCOLS = 12
RC = SEC * PCOLS
CH = 384
EPS = 1e-06
MESH = pl.DeviceIdType.MESH
NT = (((1,), (1,)), ((), ()))
LOG2E = 1.0 / math.log(2.0)


def offsets(i):
    b, c = i // 4, i % 4
    return (b // 4 + c // 2) % 2, (b + c) % 4, c


def gather_constants():
    rows = np.zeros((3, 4 * RC, 4 * RC), np.float32)
    lanes = np.zeros((3, 128, 256), np.float32)
    for k in range(3):
        for f in range(4):
            for r in range(SEC):
                for c in range(PCOLS):
                    if 0 <= c + k - 1 < PCOLS:
                        rows[k, (f * SEC + r) * PCOLS + c, (r * 4 + f) * PCOLS + c + k - 1] = 1
    for half in range(2):
        for i in range(2):
            for tap, (k, j) in enumerate(((0, 1), (1, 0), (1, 1), (2, 0))):
                for ch in range(16):
                    lanes[k, half * 64 + i * 32 + j * 16 + ch, half * 128 + i * 64 + tap * 16 + ch] = 1
    return rows, lanes.reshape(384, 256)


def kernel(
    q_hbm, k_hbm, v_hbm, qg_ref, kg_ref, noisy_ref, hw_hbm, win_hbm, bias_ref, vg_ref, w_hbm, rowsel_hbm, lanesel_hbm,
    lat_ref, dec_ref,
    q_ref, k_ref, v_ref, hw_ref, win_ref, wconv, rowsel_ref, lanesel_ref, qsrc, kvsrc, qbuf, kvbuf, sibbuf, keys, values, acc, m_s, l_s, s_a, s_b, gsrc, gbuf, hsrc, vbuf,
    noisy_s, xsrc, xrecv, xf, lhs, hid, tap, wbig, cacc, dec_s,
    ssq, sskv, ssf, sso, ssh, ssx, rq, rkv, rf, ro, rh, rx, lsem,
):
    sec, p = lax.axis_index("sec"), lax.axis_index("seq")
    z_lo, core = lax.div(sec, 2), lax.rem(sec, 2)
    part, place = lax.div(p, 32), lax.rem(p, 32)
    loads = (
        (q_hbm, q_ref), (k_hbm, k_ref), (v_hbm, v_ref), (hw_hbm, hw_ref),
        (win_hbm, win_ref), (rowsel_hbm, rowsel_ref), (lanesel_hbm, lanesel_ref), (w_hbm, wconv),
    )
    local = [
        pltpu.make_async_copy(src, dst, lsem.at[n])
        for n, (src, dst) in enumerate(loads)
    ]
    for copy in local[:4]:
        copy.start()

    place_y, place_x, place_z = lax.div(place, 16), lax.rem(lax.div(place, 4), 4), lax.rem(place, 4)
    ys = [lax.rem(place_y + n, 2) * 16 for n in range(2)]
    xs = [lax.rem(place_x + n, 4) * 4 for n in range(4)]
    zs = [lax.rem(place_z + n, 4) for n in range(4)]

    def target(h):
        return (2 * z_lo + 1 - part, h + 32 * core)

    def source(j):
        return (2 * z_lo + part, j + 32 * (1 - core))

    def head_at(i):
        dy, dx, dz = offsets(i)
        return ys[dy] + xs[dx] + zs[dz]

    def source_at(i):
        dy, dx, dz = offsets(i)
        return source(ys[dy] + xs[-dx % 4] + zs[-dz % 4])

    def peer_at(e):
        y = lax.rem(place_y + lax.div(e, 4), 2)
        x = lax.rem(place_x + 8 - e, 4)
        return (sec, y * 16 + x * 4 + place_z + 32 * part)

    sibling = (2 * z_lo + 1 - core, p)

    def beside(d):
        return lax.rem(p + SEQ + d, SEQ)

    barrier = pltpu.get_barrier_semaphore()
    for i in range(STEPS):
        pl.semaphore_signal(barrier, inc=1, device_id=source_at(i), device_id_type=MESH)
    for d in (-1, 0, 1):
        for s in range(1, SEC) if d == 0 else range(SEC):
            pl.semaphore_signal(barrier, inc=1, device_id=(lax.rem(sec + s, SEC), beside(d)), device_id_type=MESH)

    def normed(ref, gain_ref, factor, store):
        def some(t, _):
            rows = pl.ds(pl.multiple_of(t * 16, 16), 16)
            x = ref[rows, :].astype(jnp.float32)
            scale = lax.rsqrt(jnp.mean(x * x, axis=-1, keepdims=True) + EPS)
            for h in range(HEADS):
                cols = slice(h * HEAD_DIM, (h + 1) * HEAD_DIM)
                y = x[:, cols] * scale * gain_ref[:, cols]
                store(h, rows, (y if factor is None else y * factor).astype(jnp.bfloat16))
            return 0

        lax.fori_loop(0, ROWS // 16, some, 0)

    def store_q(h, rows, y):
        qsrc[h, rows, :] = y

    def store_k(h, rows, y):
        kvsrc[h, rows, :] = y

    local[0].wait()
    normed(q_ref, qg_ref, LOG2E / math.sqrt(HEAD_DIM), store_q)
    pl.semaphore_wait(barrier, STEPS + 3 * SEC - 1)
    def send_queries(j):
        for n in range(PER_QB):
            e, i = 2 * j + n // 4, j * PER_QB + n
            h = lax.rem(place_y + lax.div(e, 4), 2) * 16 + lax.rem(place_x + e, 4) * 4 + zs[n % 4]
            pltpu.make_async_remote_copy(
                src_ref=qsrc.at[h],
                dst_ref=qbuf.at[i],
                send_sem=ssq.at[j],
                recv_sem=rq.at[j],
                device_id=target(h),
                device_id_type=MESH,
            ).start()

    send_queries(0)
    for copy in local[4:]:
        copy.start()
    local[1].wait()
    normed(k_ref, kg_ref, None, store_k)
    local[2].wait()
    local[3].wait()
    for h in range(HEADS):
        cols = slice(h * HEAD_DIM, (h + 1) * HEAD_DIM)
        weighted = lax.dot_general(v_ref[:, cols], hw_ref[:, cols], NT, preferred_element_type=jnp.float32)
        kvsrc[h, pl.ds(ROWS, HALF)] = jnp.concatenate([weighted[:HALF], weighted[HALF:]], axis=1).astype(jnp.bfloat16)

    def send_chunk(g):
        for n in range(PER_CHUNK):
            y = lax.rem(place_y + lax.div(g, 4) + n // 2, 2)
            x = lax.rem(place_x + g + n, 4)
            h = y * 16 + x * 4 + zs[n]
            pltpu.make_async_remote_copy(
                src_ref=kvsrc.at[h],
                dst_ref=kvbuf.at[g * PER_CHUNK + n],
                send_sem=sskv.at[g],
                recv_sem=rkv.at[g],
                device_id=target(h),
                device_id_type=MESH,
            ).start()

    def arrived(buffer, sem):
        pltpu.make_async_copy(buffer, buffer, sem).wait()

    def chunk_of(buffer, g):
        return buffer.at[pl.ds(g * PER_CHUNK, PER_CHUNK)]

    def queries_of(buffer, j):
        return buffer.at[pl.ds(j * PER_QB, PER_QB)]

    def sent_queries(j):
        arrived(queries_of(qsrc, j), ssq.at[j])

    def sent_chunk(g):
        arrived(chunk_of(kvsrc, g), sskv.at[g])

    send_chunk(0)
    send_chunk(1)
    send_chunk(2)
    wbig[...] = jnp.zeros_like(wbig)
    local[4].wait()
    for a in range(3):
        for b in range(3):
            block = win_ref[pl.ds((a * 3 + b) * 48, 48), :]
            for i in range(2):
                for j in range(2):
                    wbig[pl.ds(a * 256 + (b + i) * 64 + j * 16, 48), pl.ds((i * 2 + j) * CH, CH)] = block
    xf[pl.ds(0, 4)] = jnp.zeros((4,) + xf.shape[1:], jnp.bfloat16)
    noisy = noisy_ref[...].T
    noisy_s[...] = jnp.concatenate([noisy[:HALF], noisy[HALF:]], axis=1)
    acc[...] = jnp.zeros_like(acc)
    l_s[...] = jnp.zeros_like(l_s)
    m_s[...] = jnp.full_like(m_s, -1e30)
    sent_queries(0)
    send_chunk(3)
    sent_chunk(0)
    send_queries(1)
    sent_chunk(1)
    send_queries(2)

    def pass_on(g):
        arrived(chunk_of(kvbuf, g), rkv.at[g])
        pltpu.make_async_remote_copy(
            src_ref=chunk_of(kvbuf, g),
            dst_ref=chunk_of(sibbuf, g),
            send_sem=ssf.at[g],
            recv_sem=rf.at[g],
            device_id=sibling,
            device_id_type=MESH,
        ).start()

    def take(g):
        arrived(chunk_of(sibbuf, g), rf.at[g])
        steps = pl.ds(g * PER_CHUNK, PER_CHUNK)
        for half in range(2):
            for n, buffer in enumerate((kvbuf, sibbuf)):
                keys[g, pl.ds((half * 2 + n) * KC // 4, KC // 4), :] = buffer[steps, pl.ds(half * HALF, HALF)].reshape(KC // 4, HEAD_DIM)
        both = jnp.concatenate([buffer[steps, pl.ds(ROWS, HALF)].reshape(KC // 4, 128) for buffer in (kvbuf, sibbuf)], axis=0).T
        values[g, :, pl.ds(0, KC // 2)] = both[:64]
        values[g, :, pl.ds(KC // 2, KC // 2)] = both[64:]

    def score(g, j, dst):
        q = qbuf[pl.ds(j * PER_QB, PER_QB)].reshape(QB, HEAD_DIM)
        dst[...] = lax.dot_general(keys[g], q, NT, preferred_element_type=jnp.float32)

    def update(g, j, src):
        s = src[...]
        m_old = m_s[j]
        m_new = jnp.maximum(m_old, jnp.max(s, axis=0, keepdims=True))
        m_s[j] = m_new
        alpha = jnp.exp2(m_old - m_new)
        e = jnp.exp2(s - m_new[:1])
        l_s[j] = l_s[j] * alpha + jnp.sum(e.reshape(KC // 8, 8, QB), axis=0)
        acc[j] = acc[j] * alpha[:1] + jnp.dot(values[g], e.astype(jnp.bfloat16), preferred_element_type=jnp.float32)

    def give_back(j):
        total = jnp.sum(l_s[j], axis=0, keepdims=True)
        velocity = (acc[j] * (1.0 / total)).T
        for u in range(PER_QB // 4):
            e = j * (PER_QB // 4) + u
            for dz in range(4):
                rows = velocity[(u * 4 + dz) * ROWS : (u * 4 + dz + 1) * ROWS]
                gsrc[e, dz] = jnp.concatenate([rows[:HALF], rows[HALF:]], axis=1).astype(jnp.bfloat16)

            @pl.when(e == 0)
            def _():
                gbuf[0] = gsrc[0]

            @pl.when(e > 0)
            def _():
                pltpu.make_async_remote_copy(
                    src_ref=gsrc.at[e], dst_ref=gbuf.at[e], send_sem=sso, recv_sem=ro, device_id=peer_at(e), device_id_type=MESH
                ).start()

    for g in range(EARLY):
        pass_on(g)
        if g == 2:
            sent_chunk(2)
            send_queries(3)
    for g in range(EARLY):
        take(g)
    arrived(queries_of(qbuf, 0), rq.at[0])

    n_steps = CHUNKS * N_QB
    n_early = EARLY * N_QB

    def place_of(t):
        early = t < n_early
        major, minor = lax.div(t, 4), lax.rem(t, 4)
        return jnp.where(early, minor, major), jnp.where(early, major, lax.rem(2 * minor + 1, 5))

    def step(t, now, then):
        g, j = place_of(t)
        after = jnp.minimum(t + 1, n_steps - 1)
        g_after, j_after = place_of(after)
        starts = lax.rem(t, 4) == 0

        @pl.when(t == 0)
        def _():
            sent_chunk(3)
            send_chunk(4)

        @pl.when(jnp.logical_and(starts, jnp.logical_and(t > 0, t < n_early)))
        def _():
            sent_queries(j)
            send_chunk(j + 4)

        @pl.when(jnp.logical_and(lax.rem(t, 4) == 3, t + 1 < n_early))
        def _():
            arrived(queries_of(qbuf, j_after), rq.at[j_after])

        @pl.when(jnp.logical_and(lax.rem(t, 4) == 3, jnp.logical_and(t + 1 >= n_early, t + 1 < n_steps)))
        def _():
            take(g_after)

        score(g_after, j_after, then)
        update(g, j, now)

        @pl.when(t >= n_steps - N_QB)
        def _():
            give_back(j)

        @pl.when(jnp.logical_or(t == n_early - 2, jnp.logical_and(lax.rem(t, 4) == 1, jnp.logical_and(t > n_early, t < n_steps - 4))))
        def _():
            pass_on(lax.div(t + 3, 4))

    score(0, 0, s_a)

    def two_steps(n, _):
        step(2 * n, s_a, s_b)
        step(2 * n + 1, s_b, s_a)
        return 0

    lax.fori_loop(0, n_steps // 2, two_steps, 0)

    arrived(gbuf.at[pl.ds(1, PEERS - 1)], ro)
    hsrc[...] = jnp.sum(gbuf[...].astype(jnp.float32), axis=0).astype(jnp.bfloat16)
    for dz in range(4):
        pltpu.make_async_remote_copy(
            src_ref=hsrc.at[dz],
            dst_ref=vbuf.at[dz],
            send_sem=ssh,
            recv_sem=rh,
            device_id=source(ys[0] + xs[0] + zs[-dz % 4]),
            device_id_type=MESH,
        ).start()
    arrived(vbuf, rh)
    latents = noisy_s[...] + jnp.sum(vbuf[...].astype(jnp.float32), axis=0)
    patches = latents.astype(jnp.bfloat16)
    xsrc[...] = patches
    xrecv[SEC + sec] = patches
    for d in (-1, 0, 1):
        for s in range(1, SEC) if d == 0 else range(SEC):
            pltpu.make_async_remote_copy(
                src_ref=xsrc,
                dst_ref=xrecv.at[(1 - d) * SEC + sec],
                send_sem=ssx,
                recv_sem=rx,
                device_id=(lax.rem(sec + s, SEC), beside(d)),
                device_id_type=MESH,
            ).start()
    lat_ref[...] = jnp.concatenate([latents[:, :64], latents[:, 64:]], axis=0).T
    arrived(xrecv.at[pl.ds(0, 3 * SEC - 1)], rx)

    local[5].wait()
    local[6].wait()
    for d in range(3):
        got = xrecv[pl.ds(d * SEC, SEC)].reshape(SEC * HALF, 128)
        shifted = [jnp.dot(rowsel_ref[k], got, preferred_element_type=jnp.float32).astype(jnp.bfloat16) for k in range(3)]
        rows = jnp.dot(jnp.concatenate(shifted, axis=1), lanesel_ref[...], preferred_element_type=jnp.float32)
        if d == 0:
            rows = jnp.where(p == 0, 0.0, rows)
        if d == 2:
            rows = jnp.where(p == SEQ - 1, 0.0, rows)
        rows = rows.astype(jnp.bfloat16)
        for f in range(8):
            xf[4 + f, d] = rows[f % 4 * RC : (f % 4 + 1) * RC, f // 4 * 128 : (f // 4 + 1) * 128]
    for l in range(2):
        for f in range(4):
            for a in range(3):
                for n in range(2):
                    lhs[pl.ds((l * 4 + f) * RC, RC), pl.ds(a * 256 + n * 128, 128)] = xf[2 * sec + f + a, l + n]
    row = lax.broadcasted_iota(jnp.int32, (RC, CH), 0)
    is_first = functools.reduce(jnp.logical_or, [row == r * PCOLS for r in range(SEC)])
    is_last = functools.reduce(jnp.logical_or, [row == r * PCOLS + PCOLS - 1 for r in range(SEC)])
    bias, gain = bias_ref[...].reshape(1, CH), vg_ref[...].reshape(1, CH)

    def convolve(n):
        cols = pl.ds(n * CH, CH)
        hid[:, cols] = jnp.dot(lhs[...], wbig[:, cols], preferred_element_type=jnp.float32) + bias

    def activate(n):
        i, j = n // 2, n % 2
        for l in range(2):
            for f in range(4):
                y = 2 * l + i
                x = hid[pl.ds((l * 4 + f) * RC, RC), pl.ds(n * CH, CH)].astype(jnp.bfloat16).astype(jnp.float32)
                x = x * lax.rsqrt(jnp.mean(x * x, axis=-1, keepdims=True) + EPS) * gain
                x = 0.5 * x
                x = x + x * jnp.tanh(x)
                outside = [sec == 0] * (f < 2) + [p == 0] * (y == 0) + [p == SEQ - 1] * (y == 3)
                if outside:
                    x = jnp.where(functools.reduce(jnp.logical_or, outside), 0.0, x)
                tap[f, y, :, pl.ds((1 + j) * CH, CH)] = x.astype(jnp.bfloat16)
                if j == 0:
                    x = jnp.where(is_last, 0.0, pltpu.roll(x, RC - 1, 0))
                    tap[f, y, :, pl.ds(3 * CH, CH)] = x.astype(jnp.bfloat16)
                else:
                    x = jnp.where(is_first, 0.0, pltpu.roll(x, 1, 0))
                    tap[f, y, :, pl.ds(0, CH)] = x.astype(jnp.bfloat16)

    convolve(0)
    for n in range(4):
        if n < 3:
            convolve(n + 1)
        activate(n)

    local[7].wait()
    def one_tap(t):
        a, b = t // 3, t % 3
        block = tap[pl.ds(a, 2), pl.ds(b, 2)].reshape(4 * RC, 4 * CH)
        both = jnp.concatenate([block[:, : 3 * CH], block[:, CH:]], axis=0)
        return jnp.dot(both, wconv[t], preferred_element_type=jnp.float32)

    cacc[...] = one_tap(0) + one_tap(1) + one_tap(2)
    cacc[...] += one_tap(3) + one_tap(4) + one_tap(5)
    cacc[...] += one_tap(6) + one_tap(7) + one_tap(8)
    for f in range(2):
        for y in range(2):
            rows = pl.ds((y * 4 + 2 + f) * RC, RC)
            for j in range(2):
                hidden = hid[rows, pl.ds(((1 - y) * 2 + j) * CH, CH)].astype(jnp.bfloat16).astype(jnp.float32)
                out = hidden + cacc[pl.ds(((j * 2 + f) * 2 + y) * RC, RC), :]
                for r in range(SEC):
                    for n in range(CH // 128):
                        part_out = out[r * PCOLS : (r + 1) * PCOLS, n * 128 : (n + 1) * 128]
                        dec_s[r, f, y, n, pl.ds(j, PCOLS, 2), :] = part_out
            for r in range(SEC):
                for n in range(CH // 128):
                    dec_ref[r, f, y, :, pl.ds(n * 128, 128)] = dec_s[r, f, y, n].astype(jnp.bfloat16)

    for g in range(4, CHUNKS):
        sent_chunk(g)
    arrived(gsrc.at[pl.ds(1, PEERS - 1)], sso)
    arrived(hsrc, ssh)
    arrived(xrecv.at[pl.ds(0, 3 * SEC - 1)], ssx)

    def sent(g, _):
        arrived(chunk_of(kvbuf, g), ssf.at[g])
        return 0

    lax.fori_loop(0, CHUNKS, sent, 0)


def hand_on(lat_ref, dec_ref, lat_out, dec_out):
    lat_out[...] = lat_ref[...]
    dec_out[...] = dec_ref[...]


def shards(
    queries, keys, values, query_gain, key_gain, noisy, head_weight, conv_in_weight, conv_in_bias, vae_gain, conv_weight
):
    rowsel, lanesel = gather_constants()
    vmem = pl.BlockSpec(memory_space=pltpu.VMEM)
    anywhere = pl.BlockSpec(memory_space=pl.ANY)
    bf16, f32, dma = jnp.bfloat16, jnp.float32, pltpu.SemaphoreType.DMA
    latents, decoded = pl.pallas_call(
        kernel,
        out_shape=(jax.ShapeDtypeStruct((64, ROWS), f32), jax.ShapeDtypeStruct((SEC, 2, 2, 2 * PCOLS, CH), bf16)),
        in_specs=[anywhere] * 3 + [vmem] * 3 + [anywhere] * 2 + [vmem] * 2 + [anywhere] * 3,
        out_specs=(vmem, vmem),
        scratch_shapes=[
            *[pltpu.VMEM((ROWS, HEADS * HEAD_DIM), bf16)] * 3,
            pltpu.VMEM((64, HEADS * HEAD_DIM), bf16),
            pltpu.VMEM((432, CH), bf16),
            pltpu.VMEM((9, 3 * CH, CH), bf16),
            pltpu.VMEM((3, 4 * RC, 4 * RC), bf16),
            pltpu.VMEM((384, 256), bf16),
            pltpu.VMEM((HEADS, ROWS, HEAD_DIM), bf16),
            pltpu.VMEM((HEADS, KV_ROWS, HEAD_DIM), bf16),
            pltpu.VMEM((STEPS, ROWS, HEAD_DIM), bf16),
            pltpu.VMEM((STEPS, KV_ROWS, HEAD_DIM), bf16),
            pltpu.VMEM((STEPS, KV_ROWS, HEAD_DIM), bf16),
            pltpu.VMEM((CHUNKS, KC, HEAD_DIM), bf16),
            pltpu.VMEM((CHUNKS, 64, KC), bf16),
            pltpu.VMEM((N_QB, 64, QB), f32),
            pltpu.VMEM((N_QB, 8, QB), f32),
            pltpu.VMEM((N_QB, 8, QB), f32),
            pltpu.VMEM((KC, QB), f32),
            pltpu.VMEM((KC, QB), f32),
            *[pltpu.VMEM((PEERS, 4, HALF, 128), bf16)] * 2,
            *[pltpu.VMEM((4, HALF, 128), bf16)] * 2,
            pltpu.VMEM((HALF, 128), f32),
            pltpu.VMEM((HALF, 128), bf16),
            pltpu.VMEM((3 * SEC, HALF, 128), bf16),
            pltpu.VMEM((12, 3, RC, 128), bf16),
            pltpu.VMEM((8 * RC, 768), bf16),
            pltpu.VMEM((8 * RC, 4 * CH), f32),
            pltpu.VMEM((4, 4, RC, 4 * CH), bf16),
            pltpu.VMEM((768, 4 * CH), bf16),
            pltpu.VMEM((8 * RC, CH), f32),
            pltpu.VMEM((SEC, 2, 2, CH // 128, 2 * PCOLS, 128), f32),
            dma((N_QB,)), dma((CHUNKS,)), dma((CHUNKS,)), dma, dma, dma, dma((N_QB,)), dma((CHUNKS,)), dma((CHUNKS,)), dma, dma, dma, dma((8,)),
        ],
        compiler_params=pltpu.CompilerParams(collective_id=0, has_side_effects=True, vmem_limit_bytes=56 * 2**20),
        name="step",
    )(
        queries[0],
        keys[0],
        values[0],
        query_gain.reshape(1, -1),
        key_gain.reshape(1, -1),
        noisy[0].T,
        head_weight.T,
        conv_in_weight.reshape(432, CH),
        conv_in_bias,
        vae_gain,
        conv_weight.reshape(9, 3 * CH, CH),
        jnp.asarray(rowsel, bf16),
        jnp.asarray(lanesel, bf16),
    )
    latents, decoded = pl.pallas_call(
        hand_on,
        out_shape=(jax.ShapeDtypeStruct(latents.shape, f32), jax.ShapeDtypeStruct(decoded.shape, bf16)),
        in_specs=[vmem] * 2,
        out_specs=(vmem, vmem),
        name="hand_on",
    )(latents, decoded)
    return latents.T[None], decoded


def solution(mesh):
    placed = (
        P("sec", "seq", None),
        P("sec", "seq", None),
        P("sec", "seq", None),
        P(),
        P(),
        P("sec", "seq", None),
        P(),
        P(),
        P(),
        P(),
        P(),
    )
    return jax.shard_map(
        shards,
        mesh=mesh,
        in_specs=placed,
        out_specs=(P("sec", "seq", None), P(None, "sec", "seq", None, None)),
        check_vma=False,
    )
```

```python
import functools
import math

import jax
import jax.numpy as jnp
import numpy as np
from jax import lax
from jax.experimental import pallas as pl
from jax.experimental.pallas import tpu as pltpu
from jax.sharding import PartitionSpec as P

HEADS = 32
HEAD_DIM = 128
ROWS = 96
HALF = ROWS // 2
SEQ = 64
SEC = 4
STEPS = 32
PER_CHUNK = 4
CHUNKS = STEPS // PER_CHUNK
EARLY = CHUNKS // 2
PER_QB = 8
QB = PER_QB * ROWS
N_QB = STEPS // PER_QB
PEERS = STEPS // 4
KC = 2 * PER_CHUNK * ROWS
KV_ROWS = ROWS + HALF
PCOLS = 12
RC = SEC * PCOLS
CH = 384
EPS = 1e-06
MESH = pl.DeviceIdType.MESH
NT = (((1,), (1,)), ((), ()))
LOG2E = 1.0 / math.log(2.0)


def offsets(i):
    b, c = i // 4, i % 4
    return (b // 4 + c // 2) % 2, (b + c) % 4, c


def gather_constants():
    rows = np.zeros((3, 4 * RC, 4 * RC), np.float32)
    lanes = np.zeros((3, 128, 256), np.float32)
    for k in range(3):
        for f in range(4):
            for r in range(SEC):
                for c in range(PCOLS):
                    if 0 <= c + k - 1 < PCOLS:
                        rows[k, (f * SEC + r) * PCOLS + c, (r * 4 + f) * PCOLS + c + k - 1] = 1
    for half in range(2):
        for i in range(2):
            for tap, (k, j) in enumerate(((0, 1), (1, 0), (1, 1), (2, 0))):
                for ch in range(16):
                    lanes[k, half * 64 + i * 32 + j * 16 + ch, half * 128 + i * 64 + tap * 16 + ch] = 1
    return rows, lanes.reshape(384, 256)


def kernel(
    q_hbm, k_hbm, v_hbm, qg_ref, kg_ref, noisy_ref, hw_hbm, win_hbm, bias_ref, vg_ref, w_hbm, rowsel_hbm, lanesel_hbm,
    lat_ref, dec_ref,
    q_ref, k_ref, v_ref, hw_ref, win_ref, wconv, rowsel_ref, lanesel_ref, qsrc, kvsrc, qbuf, kvbuf, sibbuf, keys, values, acc, m_s, l_s, s_a, s_b, gsrc, gbuf, hsrc, vbuf,
    noisy_s, xsrc, xrecv, xf, lhs, hid, tap, wbig, cacc, dec_s,
    ssq, sskv, ssf, sso, ssh, ssx, rq, rkv, rf, ro, rh, rx, lsem,
):
    sec, p = lax.axis_index("sec"), lax.axis_index("seq")
    z_lo, core = lax.div(sec, 2), lax.rem(sec, 2)
    part, place = lax.div(p, 32), lax.rem(p, 32)
    loads = (
        (q_hbm, q_ref), (k_hbm, k_ref), (v_hbm, v_ref), (hw_hbm, hw_ref),
        (win_hbm, win_ref), (rowsel_hbm, rowsel_ref), (lanesel_hbm, lanesel_ref), (w_hbm, wconv),
    )
    local = [
        pltpu.make_async_copy(src, dst, lsem.at[n])
        for n, (src, dst) in enumerate(loads)
    ]
    for copy in local[:4]:
        copy.start()

    place_y, place_x, place_z = lax.div(place, 16), lax.rem(lax.div(place, 4), 4), lax.rem(place, 4)
    ys = [lax.rem(place_y + n, 2) * 16 for n in range(2)]
    xs = [lax.rem(place_x + n, 4) * 4 for n in range(4)]
    zs = [lax.rem(place_z + n, 4) for n in range(4)]

    def target(h):
        return (2 * z_lo + 1 - part, h + 32 * core)

    def source(j):
        return (2 * z_lo + part, j + 32 * (1 - core))

    def head_at(i):
        dy, dx, dz = offsets(i)
        return ys[dy] + xs[dx] + zs[dz]

    def source_at(i):
        dy, dx, dz = offsets(i)
        return source(ys[dy] + xs[-dx % 4] + zs[-dz % 4])

    def peer_at(e):
        y = lax.rem(place_y + lax.div(e, 4), 2)
        x = lax.rem(place_x + 8 - e, 4)
        return (sec, y * 16 + x * 4 + place_z + 32 * part)

    sibling = (2 * z_lo + 1 - core, p)

    def beside(d):
        return lax.rem(p + SEQ + d, SEQ)

    barrier = pltpu.get_barrier_semaphore()
    for i in range(STEPS):
        pl.semaphore_signal(barrier, inc=1, device_id=source_at(i), device_id_type=MESH)
    for d in (-1, 0, 1):
        for s in range(1, SEC) if d == 0 else range(SEC):
            pl.semaphore_signal(barrier, inc=1, device_id=(lax.rem(sec + s, SEC), beside(d)), device_id_type=MESH)

    def normed(ref, gain_ref, factor, store):
        def some(t, _):
            rows = pl.ds(pl.multiple_of(t * 16, 16), 16)
            x = ref[rows, :].astype(jnp.float32)
            scale = lax.rsqrt(jnp.mean(x * x, axis=-1, keepdims=True) + EPS)
            for h in range(HEADS):
                cols = slice(h * HEAD_DIM, (h + 1) * HEAD_DIM)
                y = x[:, cols] * scale * gain_ref[:, cols]
                store(h, rows, (y if factor is None else y * factor).astype(jnp.bfloat16))
            return 0

        lax.fori_loop(0, ROWS // 16, some, 0)

    def store_q(h, rows, y):
        qsrc[h, rows, :] = y

    def store_k(h, rows, y):
        kvsrc[h, rows, :] = y

    local[0].wait()
    normed(q_ref, qg_ref, LOG2E / math.sqrt(HEAD_DIM), store_q)
    pl.semaphore_wait(barrier, STEPS + 3 * SEC - 1)
    def send_queries(j):
        for n in range(PER_QB):
            e, i = 2 * j + n // 4, j * PER_QB + n
            h = lax.rem(place_y + lax.div(e, 4), 2) * 16 + lax.rem(place_x + e, 4) * 4 + zs[n % 4]
            pltpu.make_async_remote_copy(
                src_ref=qsrc.at[h],
                dst_ref=qbuf.at[i],
                send_sem=ssq.at[j],
                recv_sem=rq.at[j],
                device_id=target(h),
                device_id_type=MESH,
            ).start()

    send_queries(0)
    for copy in local[4:]:
        copy.start()
    local[1].wait()
    normed(k_ref, kg_ref, None, store_k)
    local[2].wait()
    local[3].wait()
    for h in range(HEADS):
        cols = slice(h * HEAD_DIM, (h + 1) * HEAD_DIM)
        weighted = lax.dot_general(v_ref[:, cols], hw_ref[:, cols], NT, preferred_element_type=jnp.float32)
        kvsrc[h, pl.ds(ROWS, HALF)] = jnp.concatenate([weighted[:HALF], weighted[HALF:]], axis=1).astype(jnp.bfloat16)

    def send_chunk(g):
        for n in range(PER_CHUNK):
            y = lax.rem(place_y + lax.div(g, 4) + n // 2, 2)
            x = lax.rem(place_x + g + n, 4)
            h = y * 16 + x * 4 + zs[n]
            pltpu.make_async_remote_copy(
                src_ref=kvsrc.at[h],
                dst_ref=kvbuf.at[g * PER_CHUNK + n],
                send_sem=sskv.at[g],
                recv_sem=rkv.at[g],
                device_id=target(h),
                device_id_type=MESH,
            ).start()

    def arrived(buffer, sem):
        pltpu.make_async_copy(buffer, buffer, sem).wait()

    def chunk_of(buffer, g):
        return buffer.at[pl.ds(g * PER_CHUNK, PER_CHUNK)]

    def queries_of(buffer, j):
        return buffer.at[pl.ds(j * PER_QB, PER_QB)]

    def sent_queries(j):
        arrived(queries_of(qsrc, j), ssq.at[j])

    def sent_chunk(g):
        arrived(chunk_of(kvsrc, g), sskv.at[g])

    send_chunk(0)
    send_chunk(1)
    wbig[...] = jnp.zeros_like(wbig)
    local[4].wait()
    for a in range(3):
        for b in range(3):
            block = win_ref[pl.ds((a * 3 + b) * 48, 48), :]
            for i in range(2):
                for j in range(2):
                    wbig[pl.ds(a * 256 + (b + i) * 64 + j * 16, 48), pl.ds((i * 2 + j) * CH, CH)] = block
    xf[pl.ds(0, 4)] = jnp.zeros((4,) + xf.shape[1:], jnp.bfloat16)
    noisy = noisy_ref[...].T
    noisy_s[...] = jnp.concatenate([noisy[:HALF], noisy[HALF:]], axis=1)
    acc[...] = jnp.zeros_like(acc)
    l_s[...] = jnp.zeros_like(l_s)
    m_s[...] = jnp.full_like(m_s, -1e30)

    def pass_on(g):
        arrived(chunk_of(kvbuf, g), rkv.at[g])
        pltpu.make_async_remote_copy(
            src_ref=chunk_of(kvbuf, g),
            dst_ref=chunk_of(sibbuf, g),
            send_sem=ssf.at[g],
            recv_sem=rf.at[g],
            device_id=sibling,
            device_id_type=MESH,
        ).start()

    def take(g):
        arrived(chunk_of(sibbuf, g), rf.at[g])
        steps = pl.ds(g * PER_CHUNK, PER_CHUNK)
        for half in range(2):
            for n, buffer in enumerate((kvbuf, sibbuf)):
                keys[g, pl.ds((half * 2 + n) * KC // 4, KC // 4), :] = buffer[steps, pl.ds(half * HALF, HALF)].reshape(KC // 4, HEAD_DIM)
        both = jnp.concatenate([buffer[steps, pl.ds(ROWS, HALF)].reshape(KC // 4, 128) for buffer in (kvbuf, sibbuf)], axis=0).T
        values[g, :, pl.ds(0, KC // 2)] = both[:64]
        values[g, :, pl.ds(KC // 2, KC // 2)] = both[64:]

    def score(g, j, dst):
        q = qbuf[pl.ds(j * PER_QB, PER_QB)].reshape(QB, HEAD_DIM)
        dst[...] = lax.dot_general(keys[g], q, NT, preferred_element_type=jnp.float32)

    def update(g, j, src):
        s = src[...]
        m_old = m_s[j]
        m_new = jnp.maximum(m_old, jnp.max(s, axis=0, keepdims=True))
        m_s[j] = m_new
        alpha = jnp.exp2(m_old - m_new)
        e = jnp.exp2(s - m_new[:1])
        l_s[j] = l_s[j] * alpha + jnp.sum(e.reshape(KC // 8, 8, QB), axis=0)
        acc[j] = acc[j] * alpha[:1] + jnp.dot(values[g], e.astype(jnp.bfloat16), preferred_element_type=jnp.float32)

    def give_back(j):
        total = jnp.sum(l_s[j], axis=0, keepdims=True)
        velocity = (acc[j] * (1.0 / total)).T
        for u in range(PER_QB // 4):
            e = j * (PER_QB // 4) + u
            for dz in range(4):
                rows = velocity[(u * 4 + dz) * ROWS : (u * 4 + dz + 1) * ROWS]
                gsrc[e, dz] = jnp.concatenate([rows[:HALF], rows[HALF:]], axis=1).astype(jnp.bfloat16)

            @pl.when(e == 0)
            def _():
                gbuf[0] = gsrc[0]

            @pl.when(e > 0)
            def _():
                pltpu.make_async_remote_copy(
                    src_ref=gsrc.at[e], dst_ref=gbuf.at[e], send_sem=sso, recv_sem=ro, device_id=peer_at(e), device_id_type=MESH
                ).start()

    arrived(queries_of(qbuf, 0), rq.at[0])
    send_chunk(2)
    for g in range(EARLY):
        pass_on(g)
        if g == 0:
            send_chunk(3)
        else:
            send_queries(g)
    for g in range(EARLY):
        take(g)

    n_steps = CHUNKS * N_QB
    n_early = EARLY * N_QB

    def place_of(t):
        early = t < n_early
        major, minor = lax.div(t, 4), lax.rem(t, 4)
        return jnp.where(early, minor, major), jnp.where(early, major, lax.rem(2 * minor + 1, 5))

    def step(t, now, then):
        g, j = place_of(t)
        after = jnp.minimum(t + 1, n_steps - 1)
        g_after, j_after = place_of(after)

        @pl.when(jnp.logical_and(lax.rem(t, 4) == 3, t + 1 < n_early))
        def _():
            arrived(queries_of(qbuf, j_after), rq.at[j_after])

            @pl.when(t == 3)
            def _():
                send_chunk(4)

            @pl.when(t == n_early - 5)
            def _():
                send_chunk(5)

        @pl.when(jnp.logical_and(lax.rem(t, 4) == 3, jnp.logical_and(t + 1 >= n_early, t + 1 < n_steps)))
        def _():
            take(g_after)

        score(g_after, j_after, then)
        update(g, j, now)

        @pl.when(t >= n_steps - N_QB)
        def _():
            give_back(j)

        @pl.when(jnp.logical_or(t == n_early - 2, jnp.logical_and(lax.rem(t, 4) == 1, jnp.logical_and(t > n_early, t < n_steps - 4))))
        def _():
            pass_on(lax.div(t + 3, 4))

            @pl.when(t < n_early + 4)
            def _():
                send_chunk(lax.div(t + 3, 4) + 2)

    score(0, 0, s_a)

    def two_steps(n, _):
        step(2 * n, s_a, s_b)
        step(2 * n + 1, s_b, s_a)
        return 0

    lax.fori_loop(0, n_steps // 2, two_steps, 0)

    arrived(gbuf.at[pl.ds(1, PEERS - 1)], ro)
    hsrc[...] = jnp.sum(gbuf[...].astype(jnp.float32), axis=0).astype(jnp.bfloat16)
    for dz in range(4):
        pltpu.make_async_remote_copy(
            src_ref=hsrc.at[dz],
            dst_ref=vbuf.at[dz],
            send_sem=ssh,
            recv_sem=rh,
            device_id=source(ys[0] + xs[0] + zs[-dz % 4]),
            device_id_type=MESH,
        ).start()
    arrived(vbuf, rh)
    latents = noisy_s[...] + jnp.sum(vbuf[...].astype(jnp.float32), axis=0)
    patches = latents.astype(jnp.bfloat16)
    xsrc[...] = patches
    xrecv[SEC + sec] = patches
    for d in (-1, 0, 1):
        for s in range(1, SEC) if d == 0 else range(SEC):
            pltpu.make_async_remote_copy(
                src_ref=xsrc,
                dst_ref=xrecv.at[(1 - d) * SEC + sec],
                send_sem=ssx,
                recv_sem=rx,
                device_id=(lax.rem(sec + s, SEC), beside(d)),
                device_id_type=MESH,
            ).start()
    lat_ref[...] = jnp.concatenate([latents[:, :64], latents[:, 64:]], axis=0).T
    arrived(xrecv.at[pl.ds(0, 3 * SEC - 1)], rx)

    local[5].wait()
    local[6].wait()
    for d in range(3):
        got = xrecv[pl.ds(d * SEC, SEC)].reshape(SEC * HALF, 128)
        shifted = [jnp.dot(rowsel_ref[k], got, preferred_element_type=jnp.float32).astype(jnp.bfloat16) for k in range(3)]
        rows = jnp.dot(jnp.concatenate(shifted, axis=1), lanesel_ref[...], preferred_element_type=jnp.float32)
        if d == 0:
            rows = jnp.where(p == 0, 0.0, rows)
        if d == 2:
            rows = jnp.where(p == SEQ - 1, 0.0, rows)
        rows = rows.astype(jnp.bfloat16)
        for f in range(8):
            xf[4 + f, d] = rows[f % 4 * RC : (f % 4 + 1) * RC, f // 4 * 128 : (f // 4 + 1) * 128]
    for l in range(2):
        for f in range(4):
            for a in range(3):
                for n in range(2):
                    lhs[pl.ds((l * 4 + f) * RC, RC), pl.ds(a * 256 + n * 128, 128)] = xf[2 * sec + f + a, l + n]
    row = lax.broadcasted_iota(jnp.int32, (RC, CH), 0)
    is_first = functools.reduce(jnp.logical_or, [row == r * PCOLS for r in range(SEC)])
    is_last = functools.reduce(jnp.logical_or, [row == r * PCOLS + PCOLS - 1 for r in range(SEC)])
    bias, gain = bias_ref[...].reshape(1, CH), vg_ref[...].reshape(1, CH)

    def convolve(n):
        cols = pl.ds(n * CH, CH)
        hid[:, cols] = jnp.dot(lhs[...], wbig[:, cols], preferred_element_type=jnp.float32) + bias

    def activate(n):
        i, j = n // 2, n % 2
        for l in range(2):
            for f in range(4):
                y = 2 * l + i
                x = hid[pl.ds((l * 4 + f) * RC, RC), pl.ds(n * CH, CH)].astype(jnp.bfloat16).astype(jnp.float32)
                x = x * lax.rsqrt(jnp.mean(x * x, axis=-1, keepdims=True) + EPS) * gain
                x = 0.5 * x
                x = x + x * jnp.tanh(x)
                outside = [sec == 0] * (f < 2) + [p == 0] * (y == 0) + [p == SEQ - 1] * (y == 3)
                if outside:
                    x = jnp.where(functools.reduce(jnp.logical_or, outside), 0.0, x)
                tap[f, y, :, pl.ds((1 + j) * CH, CH)] = x.astype(jnp.bfloat16)
                if j == 0:
                    x = jnp.where(is_last, 0.0, pltpu.roll(x, RC - 1, 0))
                    tap[f, y, :, pl.ds(3 * CH, CH)] = x.astype(jnp.bfloat16)
                else:
                    x = jnp.where(is_first, 0.0, pltpu.roll(x, 1, 0))
                    tap[f, y, :, pl.ds(0, CH)] = x.astype(jnp.bfloat16)

    convolve(0)
    for n in range(4):
        if n < 3:
            convolve(n + 1)
        activate(n)

    local[7].wait()
    def one_tap(t):
        a, b = t // 3, t % 3
        block = tap[pl.ds(a, 2), pl.ds(b, 2)].reshape(4 * RC, 4 * CH)
        both = jnp.concatenate([block[:, : 3 * CH], block[:, CH:]], axis=0)
        return jnp.dot(both, wconv[t], preferred_element_type=jnp.float32)

    cacc[...] = one_tap(0) + one_tap(1) + one_tap(2)
    cacc[...] += one_tap(3) + one_tap(4) + one_tap(5)
    cacc[...] += one_tap(6) + one_tap(7) + one_tap(8)
    for f in range(2):
        for y in range(2):
            rows = pl.ds((y * 4 + 2 + f) * RC, RC)
            for j in range(2):
                hidden = hid[rows, pl.ds(((1 - y) * 2 + j) * CH, CH)].astype(jnp.bfloat16).astype(jnp.float32)
                out = hidden + cacc[pl.ds(((j * 2 + f) * 2 + y) * RC, RC), :]
                for r in range(SEC):
                    for n in range(CH // 128):
                        part_out = out[r * PCOLS : (r + 1) * PCOLS, n * 128 : (n + 1) * 128]
                        dec_s[r, f, y, n, pl.ds(j, PCOLS, 2), :] = part_out
            for r in range(SEC):
                for n in range(CH // 128):
                    dec_ref[r, f, y, :, pl.ds(n * 128, 128)] = dec_s[r, f, y, n].astype(jnp.bfloat16)

    for j in range(N_QB):
        sent_queries(j)
    for g in range(CHUNKS):
        sent_chunk(g)
    arrived(gsrc.at[pl.ds(1, PEERS - 1)], sso)
    arrived(hsrc, ssh)
    arrived(xrecv.at[pl.ds(0, 3 * SEC - 1)], ssx)

    def sent(g, _):
        arrived(chunk_of(kvbuf, g), ssf.at[g])
        return 0

    lax.fori_loop(0, CHUNKS, sent, 0)


def hand_on(lat_ref, dec_ref, lat_out, dec_out):
    lat_out[...] = lat_ref[...]
    dec_out[...] = dec_ref[...]


def shards(
    queries, keys, values, query_gain, key_gain, noisy, head_weight, conv_in_weight, conv_in_bias, vae_gain, conv_weight
):
    rowsel, lanesel = gather_constants()
    vmem = pl.BlockSpec(memory_space=pltpu.VMEM)
    anywhere = pl.BlockSpec(memory_space=pl.ANY)
    bf16, f32, dma = jnp.bfloat16, jnp.float32, pltpu.SemaphoreType.DMA
    latents, decoded = pl.pallas_call(
        kernel,
        out_shape=(jax.ShapeDtypeStruct((64, ROWS), f32), jax.ShapeDtypeStruct((SEC, 2, 2, 2 * PCOLS, CH), bf16)),
        in_specs=[anywhere] * 3 + [vmem] * 3 + [anywhere] * 2 + [vmem] * 2 + [anywhere] * 3,
        out_specs=(vmem, vmem),
        scratch_shapes=[
            *[pltpu.VMEM((ROWS, HEADS * HEAD_DIM), bf16)] * 3,
            pltpu.VMEM((64, HEADS * HEAD_DIM), bf16),
            pltpu.VMEM((432, CH), bf16),
            pltpu.VMEM((9, 3 * CH, CH), bf16),
            pltpu.VMEM((3, 4 * RC, 4 * RC), bf16),
            pltpu.VMEM((384, 256), bf16),
            pltpu.VMEM((HEADS, ROWS, HEAD_DIM), bf16),
            pltpu.VMEM((HEADS, KV_ROWS, HEAD_DIM), bf16),
            pltpu.VMEM((STEPS, ROWS, HEAD_DIM), bf16),
            pltpu.VMEM((STEPS, KV_ROWS, HEAD_DIM), bf16),
            pltpu.VMEM((STEPS, KV_ROWS, HEAD_DIM), bf16),
            pltpu.VMEM((CHUNKS, KC, HEAD_DIM), bf16),
            pltpu.VMEM((CHUNKS, 64, KC), bf16),
            pltpu.VMEM((N_QB, 64, QB), f32),
            pltpu.VMEM((N_QB, 8, QB), f32),
            pltpu.VMEM((N_QB, 8, QB), f32),
            pltpu.VMEM((KC, QB), f32),
            pltpu.VMEM((KC, QB), f32),
            *[pltpu.VMEM((PEERS, 4, HALF, 128), bf16)] * 2,
            *[pltpu.VMEM((4, HALF, 128), bf16)] * 2,
            pltpu.VMEM((HALF, 128), f32),
            pltpu.VMEM((HALF, 128), bf16),
            pltpu.VMEM((3 * SEC, HALF, 128), bf16),
            pltpu.VMEM((12, 3, RC, 128), bf16),
            pltpu.VMEM((8 * RC, 768), bf16),
            pltpu.VMEM((8 * RC, 4 * CH), f32),
            pltpu.VMEM((4, 4, RC, 4 * CH), bf16),
            pltpu.VMEM((768, 4 * CH), bf16),
            pltpu.VMEM((8 * RC, CH), f32),
            pltpu.VMEM((SEC, 2, 2, CH // 128, 2 * PCOLS, 128), f32),
            dma((N_QB,)), dma((CHUNKS,)), dma((CHUNKS,)), dma, dma, dma, dma((N_QB,)), dma((CHUNKS,)), dma((CHUNKS,)), dma, dma, dma, dma((8,)),
        ],
        compiler_params=pltpu.CompilerParams(collective_id=0, has_side_effects=True, vmem_limit_bytes=56 * 2**20),
        name="step",
    )(
        queries[0],
        keys[0],
        values[0],
        query_gain.reshape(1, -1),
        key_gain.reshape(1, -1),
        noisy[0].T,
        head_weight.T,
        conv_in_weight.reshape(432, CH),
        conv_in_bias,
        vae_gain,
        conv_weight.reshape(9, 3 * CH, CH),
        jnp.asarray(rowsel, bf16),
        jnp.asarray(lanesel, bf16),
    )
    latents, decoded = pl.pallas_call(
        hand_on,
        out_shape=(jax.ShapeDtypeStruct(latents.shape, f32), jax.ShapeDtypeStruct(decoded.shape, bf16)),
        in_specs=[vmem] * 2,
        out_specs=(vmem, vmem),
        name="hand_on",
    )(latents, decoded)
    return latents.T[None], decoded


def solution(mesh):
    placed = (
        P("sec", "seq", None),
        P("sec", "seq", None),
        P("sec", "seq", None),
        P(),
        P(),
        P("sec", "seq", None),
        P(),
        P(),
        P(),
        P(),
        P(),
    )
    return jax.shard_map(
        shards,
        mesh=mesh,
        in_specs=placed,
        out_specs=(P("sec", "seq", None), P(None, "sec", "seq", None, None)),
        check_vma=False,
    )
```

```python
import functools
import math

import jax
import jax.numpy as jnp
import numpy as np
from jax import lax
from jax.experimental import pallas as pl
from jax.experimental.pallas import tpu as pltpu
from jax.sharding import PartitionSpec as P

HEADS = 32
HEAD_DIM = 128
ROWS = 96
HALF = ROWS // 2
SEQ = 64
SEC = 4
STEPS = 32
PER_CHUNK = 4
CHUNKS = STEPS // PER_CHUNK
EARLY = CHUNKS // 2
PER_QB = 8
QB = PER_QB * ROWS
N_QB = STEPS // PER_QB
PEERS = STEPS // 4
KC = 2 * PER_CHUNK * ROWS
KV_ROWS = ROWS + HALF
PCOLS = 12
RC = SEC * PCOLS
CH = 384
EPS = 1e-06
MESH = pl.DeviceIdType.MESH
NT = (((1,), (1,)), ((), ()))
LOG2E = 1.0 / math.log(2.0)


def offsets(i):
    b, c = i // 4, i % 4
    return (b // 4 + c // 2) % 2, (b + c) % 4, c


def gather_constants():
    rows = np.zeros((3, 4 * RC, 4 * RC), np.float32)
    lanes = np.zeros((3, 128, 256), np.float32)
    for k in range(3):
        for f in range(4):
            for r in range(SEC):
                for c in range(PCOLS):
                    if 0 <= c + k - 1 < PCOLS:
                        rows[k, (f * SEC + r) * PCOLS + c, (r * 4 + f) * PCOLS + c + k - 1] = 1
    for half in range(2):
        for i in range(2):
            for tap, (k, j) in enumerate(((0, 1), (1, 0), (1, 1), (2, 0))):
                for ch in range(16):
                    lanes[k, half * 64 + i * 32 + j * 16 + ch, half * 128 + i * 64 + tap * 16 + ch] = 1
    return rows, lanes.reshape(384, 256)


def kernel(
    q_hbm, k_hbm, v_hbm, qg_ref, kg_ref, noisy_ref, hw_hbm, win_hbm, bias_ref, vg_ref, w_hbm, rowsel_hbm, lanesel_hbm,
    lat_ref, dec_ref,
    q_ref, k_ref, v_ref, hw_ref, win_ref, wconv, rowsel_ref, lanesel_ref, qsrc, kvsrc, qbuf, kvbuf, sibbuf, keys, values, acc, m_s, l_s, s_a, s_b, gsrc, gbuf, hsrc, vbuf,
    noisy_s, xsrc, xrecv, xf, lhs, hid, tap, wbig, cacc, dec_s,
    ssq, sskv, ssf, sso, ssh, ssx, rq, rkv, rf, ro, rh, rx, lsem,
):
    sec, p = lax.axis_index("sec"), lax.axis_index("seq")
    z_lo, core = lax.div(sec, 2), lax.rem(sec, 2)
    part, place = lax.div(p, 32), lax.rem(p, 32)
    loads = (
        (q_hbm, q_ref), (k_hbm, k_ref), (v_hbm, v_ref), (hw_hbm, hw_ref),
        (win_hbm, win_ref), (rowsel_hbm, rowsel_ref), (lanesel_hbm, lanesel_ref), (w_hbm, wconv),
    )
    local = [
        pltpu.make_async_copy(src, dst, lsem.at[n])
        for n, (src, dst) in enumerate(loads)
    ]
    for copy in local[:4]:
        copy.start()

    place_y, place_x, place_z = lax.div(place, 16), lax.rem(lax.div(place, 4), 4), lax.rem(place, 4)
    ys = [lax.rem(place_y + n, 2) * 16 for n in range(2)]
    xs = [lax.rem(place_x + n, 4) * 4 for n in range(4)]
    zs = [lax.rem(place_z + n, 4) for n in range(4)]

    def target(h):
        return (2 * z_lo + 1 - part, h + 32 * core)

    def source(j):
        return (2 * z_lo + part, j + 32 * (1 - core))

    def head_at(i):
        dy, dx, dz = offsets(i)
        return ys[dy] + xs[dx] + zs[dz]

    def source_at(i):
        dy, dx, dz = offsets(i)
        return source(ys[dy] + xs[-dx % 4] + zs[-dz % 4])

    def peer_at(e):
        y = lax.rem(place_y + lax.div(e, 4), 2)
        x = lax.rem(place_x + 8 - e, 4)
        return (sec, y * 16 + x * 4 + place_z + 32 * part)

    sibling = (2 * z_lo + 1 - core, p)

    def beside(d):
        return lax.rem(p + SEQ + d, SEQ)

    barrier = pltpu.get_barrier_semaphore()
    for i in range(STEPS):
        pl.semaphore_signal(barrier, inc=1, device_id=source_at(i), device_id_type=MESH)
    for d in (-1, 0, 1):
        for s in range(1, SEC) if d == 0 else range(SEC):
            pl.semaphore_signal(barrier, inc=1, device_id=(lax.rem(sec + s, SEC), beside(d)), device_id_type=MESH)

    def normed(ref, gain_ref, factor, store):
        def some(t, _):
            rows = pl.ds(pl.multiple_of(t * 16, 16), 16)
            x = ref[rows, :].astype(jnp.float32)
            scale = lax.rsqrt(jnp.mean(x * x, axis=-1, keepdims=True) + EPS)
            for h in range(HEADS):
                cols = slice(h * HEAD_DIM, (h + 1) * HEAD_DIM)
                y = x[:, cols] * scale * gain_ref[:, cols]
                store(h, rows, (y if factor is None else y * factor).astype(jnp.bfloat16))
            return 0

        lax.fori_loop(0, ROWS // 16, some, 0)

    def store_q(h, rows, y):
        qsrc[h, rows, :] = y

    def store_k(h, rows, y):
        kvsrc[h, rows, :] = y

    local[0].wait()
    normed(q_ref, qg_ref, LOG2E / math.sqrt(HEAD_DIM), store_q)
    pl.semaphore_wait(barrier, STEPS + 3 * SEC - 1)
    def send_queries(j):
        for n in range(PER_QB):
            e, i = 2 * j + n // 4, j * PER_QB + n
            h = lax.rem(place_y + lax.div(e, 4), 2) * 16 + lax.rem(place_x + e, 4) * 4 + zs[n % 4]
            pltpu.make_async_remote_copy(
                src_ref=qsrc.at[h],
                dst_ref=qbuf.at[i],
                send_sem=ssq.at[j],
                recv_sem=rq.at[j],
                device_id=target(h),
                device_id_type=MESH,
            ).start()

    send_queries(0)
    for copy in local[4:]:
        copy.start()
    local[1].wait()
    normed(k_ref, kg_ref, None, store_k)
    local[2].wait()
    local[3].wait()
    for h in range(HEADS):
        cols = slice(h * HEAD_DIM, (h + 1) * HEAD_DIM)
        weighted = lax.dot_general(v_ref[:, cols], hw_ref[:, cols], NT, preferred_element_type=jnp.float32)
        kvsrc[h, pl.ds(ROWS, HALF)] = jnp.concatenate([weighted[:HALF], weighted[HALF:]], axis=1).astype(jnp.bfloat16)

    def send_chunk(g):
        for n in range(PER_CHUNK):
            y = lax.rem(place_y + lax.div(g, 4) + n // 2, 2)
            x = lax.rem(place_x + g + n, 4)
            h = y * 16 + x * 4 + zs[n]
            pltpu.make_async_remote_copy(
                src_ref=kvsrc.at[h],
                dst_ref=kvbuf.at[g * PER_CHUNK + n],
                send_sem=sskv.at[g],
                recv_sem=rkv.at[g],
                device_id=target(h),
                device_id_type=MESH,
            ).start()

    def arrived(buffer, sem):
        pltpu.make_async_copy(buffer, buffer, sem).wait()

    def chunk_of(buffer, g):
        return buffer.at[pl.ds(g * PER_CHUNK, PER_CHUNK)]

    def queries_of(buffer, j):
        return buffer.at[pl.ds(j * PER_QB, PER_QB)]

    def sent_queries(j):
        arrived(queries_of(qsrc, j), ssq.at[j])

    def sent_chunk(g):
        arrived(chunk_of(kvsrc, g), sskv.at[g])

    send_chunk(0)
    send_chunk(1)
    send_chunk(2)
    send_chunk(3)
    wbig[...] = jnp.zeros_like(wbig)
    local[4].wait()
    for a in range(3):
        for b in range(3):
            block = win_ref[pl.ds((a * 3 + b) * 48, 48), :]
            for i in range(2):
                for j in range(2):
                    wbig[pl.ds(a * 256 + (b + i) * 64 + j * 16, 48), pl.ds((i * 2 + j) * CH, CH)] = block
    xf[pl.ds(0, 4)] = jnp.zeros((4,) + xf.shape[1:], jnp.bfloat16)
    noisy = noisy_ref[...].T
    noisy_s[...] = jnp.concatenate([noisy[:HALF], noisy[HALF:]], axis=1)
    acc[...] = jnp.zeros_like(acc)
    l_s[...] = jnp.zeros_like(l_s)
    m_s[...] = jnp.full_like(m_s, -1e30)
    sent_queries(0)
    send_queries(1)
    sent_chunk(0)
    sent_chunk(1)
    send_queries(2)

    def pass_on(g):
        arrived(chunk_of(kvbuf, g), rkv.at[g])
        pltpu.make_async_remote_copy(
            src_ref=chunk_of(kvbuf, g),
            dst_ref=chunk_of(sibbuf, g),
            send_sem=ssf.at[g],
            recv_sem=rf.at[g],
            device_id=sibling,
            device_id_type=MESH,
        ).start()

    def take(g):
        arrived(chunk_of(sibbuf, g), rf.at[g])
        steps = pl.ds(g * PER_CHUNK, PER_CHUNK)
        for half in range(2):
            for n, buffer in enumerate((kvbuf, sibbuf)):
                keys[g, pl.ds((half * 2 + n) * KC // 4, KC // 4), :] = buffer[steps, pl.ds(half * HALF, HALF)].reshape(KC // 4, HEAD_DIM)
        both = jnp.concatenate([buffer[steps, pl.ds(ROWS, HALF)].reshape(KC // 4, 128) for buffer in (kvbuf, sibbuf)], axis=0).T
        values[g, :, pl.ds(0, KC // 2)] = both[:64]
        values[g, :, pl.ds(KC // 2, KC // 2)] = both[64:]

    def score(g, j, dst):
        q = qbuf[pl.ds(j * PER_QB, PER_QB)].reshape(QB, HEAD_DIM)
        dst[...] = lax.dot_general(keys[g], q, NT, preferred_element_type=jnp.float32)

    def update(g, j, src):
        s = src[...]
        m_old = m_s[j]
        m_new = jnp.maximum(m_old, jnp.max(s, axis=0, keepdims=True))
        m_s[j] = m_new
        alpha = jnp.exp2(m_old - m_new)
        e = jnp.exp2(s - m_new[:1])
        l_s[j] = l_s[j] * alpha + jnp.sum(e.reshape(KC // 8, 8, QB), axis=0)
        acc[j] = acc[j] * alpha[:1] + jnp.dot(values[g], e.astype(jnp.bfloat16), preferred_element_type=jnp.float32)

    def give_back(j):
        total = jnp.sum(l_s[j], axis=0, keepdims=True)
        velocity = (acc[j] * (1.0 / total)).T
        for u in range(PER_QB // 4):
            e = j * (PER_QB // 4) + u
            for dz in range(4):
                rows = velocity[(u * 4 + dz) * ROWS : (u * 4 + dz + 1) * ROWS]
                gsrc[e, dz] = jnp.concatenate([rows[:HALF], rows[HALF:]], axis=1).astype(jnp.bfloat16)

            @pl.when(e == 0)
            def _():
                gbuf[0] = gsrc[0]

            @pl.when(e > 0)
            def _():
                pltpu.make_async_remote_copy(
                    src_ref=gsrc.at[e], dst_ref=gbuf.at[e], send_sem=sso, recv_sem=ro, device_id=peer_at(e), device_id_type=MESH
                ).start()

    for g in range(EARLY):
        pass_on(g)
        if g == 2:
            sent_chunk(2)
            send_queries(3)
    for g in range(EARLY):
        take(g)
    arrived(queries_of(qbuf, 0), rq.at[0])

    n_steps = CHUNKS * N_QB
    n_early = EARLY * N_QB

    def place_of(t):
        early = t < n_early
        major, minor = lax.div(t, 4), lax.rem(t, 4)
        return jnp.where(early, minor, major), jnp.where(early, major, lax.rem(2 * minor + 1, 5))

    def step(t, now, then):
        g, j = place_of(t)
        after = jnp.minimum(t + 1, n_steps - 1)
        g_after, j_after = place_of(after)
        starts = lax.rem(t, 4) == 0

        @pl.when(t == 0)
        def _():
            sent_chunk(3)
            send_chunk(4)

        @pl.when(jnp.logical_and(starts, jnp.logical_and(t > 0, t < n_early)))
        def _():
            sent_queries(j)
            send_chunk(j + 4)

        @pl.when(jnp.logical_and(lax.rem(t, 4) == 3, t + 1 < n_early))
        def _():
            arrived(queries_of(qbuf, j_after), rq.at[j_after])

        @pl.when(jnp.logical_and(lax.rem(t, 4) == 3, jnp.logical_and(t + 1 >= n_early, t + 1 < n_steps)))
        def _():
            take(g_after)

        score(g_after, j_after, then)
        update(g, j, now)

        @pl.when(t >= n_steps - N_QB)
        def _():
            give_back(j)

        @pl.when(jnp.logical_or(t == n_early - 2, jnp.logical_and(lax.rem(t, 4) == 1, jnp.logical_and(t > n_early, t < n_steps - 4))))
        def _():
            pass_on(lax.div(t + 3, 4))

    score(0, 0, s_a)

    def two_steps(n, _):
        step(2 * n, s_a, s_b)
        step(2 * n + 1, s_b, s_a)
        return 0

    lax.fori_loop(0, n_steps // 2, two_steps, 0)

    arrived(gbuf.at[pl.ds(1, PEERS - 1)], ro)
    hsrc[...] = jnp.sum(gbuf[...].astype(jnp.float32), axis=0).astype(jnp.bfloat16)
    for dz in range(4):
        pltpu.make_async_remote_copy(
            src_ref=hsrc.at[dz],
            dst_ref=vbuf.at[dz],
            send_sem=ssh,
            recv_sem=rh,
            device_id=source(ys[0] + xs[0] + zs[-dz % 4]),
            device_id_type=MESH,
        ).start()
    arrived(vbuf, rh)
    latents = noisy_s[...] + jnp.sum(vbuf[...].astype(jnp.float32), axis=0)
    patches = latents.astype(jnp.bfloat16)
    xsrc[...] = patches
    xrecv[SEC + sec] = patches
    for d in (-1, 0, 1):
        for s in range(1, SEC) if d == 0 else range(SEC):
            pltpu.make_async_remote_copy(
                src_ref=xsrc,
                dst_ref=xrecv.at[(1 - d) * SEC + sec],
                send_sem=ssx,
                recv_sem=rx,
                device_id=(lax.rem(sec + s, SEC), beside(d)),
                device_id_type=MESH,
            ).start()
    lat_ref[...] = jnp.concatenate([latents[:, :64], latents[:, 64:]], axis=0).T
    arrived(xrecv.at[pl.ds(0, 3 * SEC - 1)], rx)

    local[5].wait()
    local[6].wait()
    for d in range(3):
        got = xrecv[pl.ds(d * SEC, SEC)].reshape(SEC * HALF, 128)
        shifted = [jnp.dot(rowsel_ref[k], got, preferred_element_type=jnp.float32).astype(jnp.bfloat16) for k in range(3)]
        rows = jnp.dot(jnp.concatenate(shifted, axis=1), lanesel_ref[...], preferred_element_type=jnp.float32)
        if d == 0:
            rows = jnp.where(p == 0, 0.0, rows)
        if d == 2:
            rows = jnp.where(p == SEQ - 1, 0.0, rows)
        rows = rows.astype(jnp.bfloat16)
        for f in range(8):
            xf[4 + f, d] = rows[f % 4 * RC : (f % 4 + 1) * RC, f // 4 * 128 : (f // 4 + 1) * 128]
    for l in range(2):
        for f in range(4):
            for a in range(3):
                for n in range(2):
                    lhs[pl.ds((l * 4 + f) * RC, RC), pl.ds(a * 256 + n * 128, 128)] = xf[2 * sec + f + a, l + n]
    row = lax.broadcasted_iota(jnp.int32, (RC, CH), 0)
    is_first = functools.reduce(jnp.logical_or, [row == r * PCOLS for r in range(SEC)])
    is_last = functools.reduce(jnp.logical_or, [row == r * PCOLS + PCOLS - 1 for r in range(SEC)])
    bias, gain = bias_ref[...].reshape(1, CH), vg_ref[...].reshape(1, CH)

    def convolve(n):
        cols = pl.ds(n * CH, CH)
        hid[:, cols] = jnp.dot(lhs[...], wbig[:, cols], preferred_element_type=jnp.float32) + bias

    def activate(n):
        i, j = n // 2, n % 2
        for l in range(2):
            for f in range(4):
                y = 2 * l + i
                x = hid[pl.ds((l * 4 + f) * RC, RC), pl.ds(n * CH, CH)].astype(jnp.bfloat16).astype(jnp.float32)
                x = x * lax.rsqrt(jnp.mean(x * x, axis=-1, keepdims=True) + EPS) * gain
                x = 0.5 * x
                x = x + x * jnp.tanh(x)
                outside = [sec == 0] * (f < 2) + [p == 0] * (y == 0) + [p == SEQ - 1] * (y == 3)
                if outside:
                    x = jnp.where(functools.reduce(jnp.logical_or, outside), 0.0, x)
                tap[f, y, :, pl.ds((1 + j) * CH, CH)] = x.astype(jnp.bfloat16)
                if j == 0:
                    x = jnp.where(is_last, 0.0, pltpu.roll(x, RC - 1, 0))
                    tap[f, y, :, pl.ds(3 * CH, CH)] = x.astype(jnp.bfloat16)
                else:
                    x = jnp.where(is_first, 0.0, pltpu.roll(x, 1, 0))
                    tap[f, y, :, pl.ds(0, CH)] = x.astype(jnp.bfloat16)

    convolve(0)
    for n in range(4):
        if n < 3:
            convolve(n + 1)
        activate(n)

    local[7].wait()
    def one_tap(t):
        a, b = t // 3, t % 3
        block = tap[pl.ds(a, 2), pl.ds(b, 2)].reshape(4 * RC, 4 * CH)
        both = jnp.concatenate([block[:, : 3 * CH], block[:, CH:]], axis=0)
        return jnp.dot(both, wconv[t], preferred_element_type=jnp.float32)

    cacc[...] = one_tap(0) + one_tap(1) + one_tap(2)
    cacc[...] += one_tap(3) + one_tap(4) + one_tap(5)
    cacc[...] += one_tap(6) + one_tap(7) + one_tap(8)
    for f in range(2):
        for y in range(2):
            rows = pl.ds((y * 4 + 2 + f) * RC, RC)
            for j in range(2):
                hidden = hid[rows, pl.ds(((1 - y) * 2 + j) * CH, CH)].astype(jnp.bfloat16).astype(jnp.float32)
                out = hidden + cacc[pl.ds(((j * 2 + f) * 2 + y) * RC, RC), :]
                for r in range(SEC):
                    for n in range(CH // 128):
                        part_out = out[r * PCOLS : (r + 1) * PCOLS, n * 128 : (n + 1) * 128]
                        dec_s[r, f, y, n, pl.ds(j, PCOLS, 2), :] = part_out
            for r in range(SEC):
                for n in range(CH // 128):
                    dec_ref[r, f, y, :, pl.ds(n * 128, 128)] = dec_s[r, f, y, n].astype(jnp.bfloat16)

    for g in range(4, CHUNKS):
        sent_chunk(g)
    arrived(gsrc.at[pl.ds(1, PEERS - 1)], sso)
    arrived(hsrc, ssh)
    arrived(xrecv.at[pl.ds(0, 3 * SEC - 1)], ssx)

    def sent(g, _):
        arrived(chunk_of(kvbuf, g), ssf.at[g])
        return 0

    lax.fori_loop(0, CHUNKS, sent, 0)


def hand_on(lat_ref, dec_ref, lat_out, dec_out):
    lat_out[...] = lat_ref[...]
    dec_out[...] = dec_ref[...]


def shards(
    queries, keys, values, query_gain, key_gain, noisy, head_weight, conv_in_weight, conv_in_bias, vae_gain, conv_weight
):
    rowsel, lanesel = gather_constants()
    vmem = pl.BlockSpec(memory_space=pltpu.VMEM)
    anywhere = pl.BlockSpec(memory_space=pl.ANY)
    bf16, f32, dma = jnp.bfloat16, jnp.float32, pltpu.SemaphoreType.DMA
    latents, decoded = pl.pallas_call(
        kernel,
        out_shape=(jax.ShapeDtypeStruct((64, ROWS), f32), jax.ShapeDtypeStruct((SEC, 2, 2, 2 * PCOLS, CH), bf16)),
        in_specs=[anywhere] * 3 + [vmem] * 3 + [anywhere] * 2 + [vmem] * 2 + [anywhere] * 3,
        out_specs=(vmem, vmem),
        scratch_shapes=[
            *[pltpu.VMEM((ROWS, HEADS * HEAD_DIM), bf16)] * 3,
            pltpu.VMEM((64, HEADS * HEAD_DIM), bf16),
            pltpu.VMEM((432, CH), bf16),
            pltpu.VMEM((9, 3 * CH, CH), bf16),
            pltpu.VMEM((3, 4 * RC, 4 * RC), bf16),
            pltpu.VMEM((384, 256), bf16),
            pltpu.VMEM((HEADS, ROWS, HEAD_DIM), bf16),
            pltpu.VMEM((HEADS, KV_ROWS, HEAD_DIM), bf16),
            pltpu.VMEM((STEPS, ROWS, HEAD_DIM), bf16),
            pltpu.VMEM((STEPS, KV_ROWS, HEAD_DIM), bf16),
            pltpu.VMEM((STEPS, KV_ROWS, HEAD_DIM), bf16),
            pltpu.VMEM((CHUNKS, KC, HEAD_DIM), bf16),
            pltpu.VMEM((CHUNKS, 64, KC), bf16),
            pltpu.VMEM((N_QB, 64, QB), f32),
            pltpu.VMEM((N_QB, 8, QB), f32),
            pltpu.VMEM((N_QB, 8, QB), f32),
            pltpu.VMEM((KC, QB), f32),
            pltpu.VMEM((KC, QB), f32),
            *[pltpu.VMEM((PEERS, 4, HALF, 128), bf16)] * 2,
            *[pltpu.VMEM((4, HALF, 128), bf16)] * 2,
            pltpu.VMEM((HALF, 128), f32),
            pltpu.VMEM((HALF, 128), bf16),
            pltpu.VMEM((3 * SEC, HALF, 128), bf16),
            pltpu.VMEM((12, 3, RC, 128), bf16),
            pltpu.VMEM((8 * RC, 768), bf16),
            pltpu.VMEM((8 * RC, 4 * CH), f32),
            pltpu.VMEM((4, 4, RC, 4 * CH), bf16),
            pltpu.VMEM((768, 4 * CH), bf16),
            pltpu.VMEM((8 * RC, CH), f32),
            pltpu.VMEM((SEC, 2, 2, CH // 128, 2 * PCOLS, 128), f32),
            dma((N_QB,)), dma((CHUNKS,)), dma((CHUNKS,)), dma, dma, dma, dma((N_QB,)), dma((CHUNKS,)), dma((CHUNKS,)), dma, dma, dma, dma((8,)),
        ],
        compiler_params=pltpu.CompilerParams(collective_id=0, has_side_effects=True, vmem_limit_bytes=56 * 2**20),
        name="step",
    )(
        queries[0],
        keys[0],
        values[0],
        query_gain.reshape(1, -1),
        key_gain.reshape(1, -1),
        noisy[0].T,
        head_weight.T,
        conv_in_weight.reshape(432, CH),
        conv_in_bias,
        vae_gain,
        conv_weight.reshape(9, 3 * CH, CH),
        jnp.asarray(rowsel, bf16),
        jnp.asarray(lanesel, bf16),
    )
    latents, decoded = pl.pallas_call(
        hand_on,
        out_shape=(jax.ShapeDtypeStruct(latents.shape, f32), jax.ShapeDtypeStruct(decoded.shape, bf16)),
        in_specs=[vmem] * 2,
        out_specs=(vmem, vmem),
        name="hand_on",
    )(latents, decoded)
    return latents.T[None], decoded


def solution(mesh):
    placed = (
        P("sec", "seq", None),
        P("sec", "seq", None),
        P("sec", "seq", None),
        P(),
        P(),
        P("sec", "seq", None),
        P(),
        P(),
        P(),
        P(),
        P(),
    )
    return jax.shard_map(
        shards,
        mesh=mesh,
        in_specs=placed,
        out_specs=(P("sec", "seq", None), P(None, "sec", "seq", None, None)),
        check_vma=False,
    )
```
